128 devices in a mesh: section: 16 (over z_lo, y, core), tensor: 8 (over z_hi, x).
Axes of the slice: x: 4, y: 4, z: 4 (z_hi: 2, z_lo: 2; z = z_hi * 2 + z_lo), core: 2. Of those that a mesh axis runs over, the one named last changes fastest.
Arguments:
- grad_top: bfloat16 [2, 64, 6144], P(None, None, 'tensor'), may hold values from -6 to 6
- query: bfloat16 [16, 2, 64, 6144], P('section', None, None, 'tensor'), as said below
- keys: bfloat16 [16, 2, 64, 1024], P('section', None, None, 'tensor'), as said below
- values: bfloat16 [16, 2, 64, 1024], P('section', None, None, 'tensor'), may hold values from -6 to 6
- out_weight: bfloat16 [16, 6144, 6144], P('section', 'tensor'), may hold values from -0.078125 to 0.078125
- value_weight: bfloat16 [16, 6144, 1024], P('section', 'tensor'), may hold values from -0.046875 to 0.046875
Outputs:
- section_grads: bfloat16 [16, 2, 64, 6144], P('section', None, None, 'tensor')
- weight_grads: bfloat16 [16, 6144, 6144], P('section', 'tensor')
The draws below stay inside these ranges and needn't reach their ends.
Inputs may be any that keep to these rules, and one draw needn't show every extreme that they name: `query`: entries of order one; in some draws some queries nearly repeat an earlier key, several times over. `keys`: entries of order one.
All inputs are finite; a program needn't handle non-finite values.
Results may differ from the reference program's by a relative error of at most 0.035.
Values may be sent and summed in bfloat16 or wider, within the bound.
No kernel may reach another device: no remote copies, remote signals or barrier semaphores. Data moves between devices by JAX's collectives and lax.ppermute only.
A program may use at most 128 MiB of HBM per device.

```python
import math
import jax
import jax.numpy as jnp

D = 6144
HEAD_DIMENSION = 128
GROUP = 6
MB = 2
TOKEN_LENGTH = 64
SECTIONS = 16
KEY_VALUE_HEADS = 8
HEADS = 48


def base_keys(key):
    sub = jax.random.fold_in(key, 5)
    return jax.random.normal(sub, (SECTIONS, MB, TOKEN_LENGTH, KEY_VALUE_HEADS, HEAD_DIMENSION), jnp.float32)


def draw_keys(key, part):
    base = base_keys(key)
    return base.reshape(SECTIONS, MB, TOKEN_LENGTH, KEY_VALUE_HEADS * HEAD_DIMENSION).astype(jnp.bfloat16)


def draw_query(key, part):
    key = jax.random.fold_in(key, 7)
    fresh = jax.random.normal(key, (SECTIONS, MB, TOKEN_LENGTH, KEY_VALUE_HEADS, GROUP, HEAD_DIMENSION), jnp.float32)
    return fresh.reshape(SECTIONS, MB, TOKEN_LENGTH, KEY_VALUE_HEADS * GROUP * HEAD_DIMENSION).astype(jnp.bfloat16)


def levels(stream_key, shape, cuts, smallest, top_value):
    gain, own = 1.0, jax.random.fold_in(stream_key, 6)
    for position, blocks in cuts:
        draws = jnp.exp(jax.random.uniform(jax.random.fold_in(own, position), (blocks,), jnp.float32, smallest / len(cuts), top_value / len(cuts)))
        gain = gain * jnp.repeat(draws, shape[position] // blocks).reshape([-1 if axis == position else 1 for axis in range(len(shape))])
    return gain


def normal_values(stream_key, dims, spread, bound, shards=(), dtype=jnp.bfloat16):
    array = jax.random.normal(stream_key, dims, jnp.float32) * spread
    if len(shards) > 0:
        array = levels(stream_key, dims, shards, -0.22, 0.18) * array
    return jnp.clip(array, min=-bound, max=bound).astype(dtype)


def setup_inputs(seed: int = 0) -> dict:
    key_list = jax.random.split(jax.random.key(seed), 7)
    grad_top = normal_values(key_list[0], (MB, TOKEN_LENGTH, D), 1.0, 6.0, ((2, 8),))
    query = draw_query(jax.random.fold_in(key_list[6], 71), 0)
    keys = draw_keys(jax.random.fold_in(key_list[6], 71), 0)
    values = normal_values(key_list[3], (SECTIONS, MB, TOKEN_LENGTH, KEY_VALUE_HEADS * HEAD_DIMENSION), 1.0, 6.0, ((0, 16), (3, 8)))
    out_weight = normal_values(key_list[4], (SECTIONS, HEADS * HEAD_DIMENSION, D), D ** -0.5, 0.078125, ((0, 16), (1, 8)))
    value_weight = normal_values(key_list[5], (SECTIONS, D, KEY_VALUE_HEADS * HEAD_DIMENSION), (16 * KEY_VALUE_HEADS * HEAD_DIMENSION) ** -0.5, 0.046875, ((0, 16), (1, 8)))
    return {"grad_top": grad_top, "query": query, "keys": keys, "values": values, "out_weight": out_weight, "value_weight": value_weight}


def reference(grad_top, query, keys, values, out_weight, value_weight):
    rows_idx = jnp.arange(TOKEN_LENGTH)[:, None]
    cols_idx = jnp.arange(TOKEN_LENGTH)[None, :]
    causal = cols_idx <= rows_idx
    carry = grad_top
    grads = []
    weight_list = []
    for relay_section in reversed(range(SECTIONS)):
        arrived = []
        total = jnp.zeros((HEADS * HEAD_DIMENSION, D), jnp.float32)
        for micro_batch in range(MB):
            incoming = carry[micro_batch]
            qmat = query[relay_section, micro_batch].astype(jnp.float32).reshape(TOKEN_LENGTH, KEY_VALUE_HEADS, GROUP, HEAD_DIMENSION)
            kmat = keys[relay_section, micro_batch].astype(jnp.float32).reshape(TOKEN_LENGTH, KEY_VALUE_HEADS, HEAD_DIMENSION)
            value_matrix = values[relay_section, micro_batch].astype(jnp.float32).reshape(TOKEN_LENGTH, KEY_VALUE_HEADS, HEAD_DIMENSION)
            logits = jnp.einsum('qcgd,pcd->cgqp', qmat, kmat) * (1.0 / math.sqrt(HEAD_DIMENSION))
            logits = jnp.where(causal, logits, -jnp.inf)
            attention_probs = jax.nn.softmax(logits, axis=-1).astype(jnp.bfloat16)
            attn_grad = jnp.dot(incoming, out_weight[relay_section].T, preferred_element_type=jnp.float32).astype(jnp.bfloat16)
            attn_grad = attn_grad.reshape(TOKEN_LENGTH, KEY_VALUE_HEADS, GROUP, HEAD_DIMENSION)
            value_grad = jnp.einsum('cgqp,qcgd->pcd', attention_probs.astype(jnp.float32), attn_grad.astype(jnp.float32))
            value_grad = value_grad.astype(jnp.bfloat16).reshape(TOKEN_LENGTH, KEY_VALUE_HEADS * HEAD_DIMENSION)
            branch = jnp.dot(value_grad, value_weight[relay_section].T, preferred_element_type=jnp.float32)
            result = (incoming.astype(jnp.float32) + branch).astype(jnp.bfloat16)
            mixed_values = jnp.einsum('ovuf,foa->uova', attention_probs.astype(jnp.float32), value_matrix)
            mixed_values = mixed_values.astype(jnp.bfloat16).reshape(TOKEN_LENGTH, HEADS * HEAD_DIMENSION)
            total = total + jnp.dot(mixed_values.T, incoming, preferred_element_type=jnp.float32)
            arrived.append(result)
        carry = jnp.stack(arrived)
        grads.insert(0, carry)
        weight_list.insert(0, total.astype(jnp.bfloat16))
    return (jnp.stack(grads), jnp.stack(weight_list))
```

```python
import math

import jax
import jax.numpy as jnp
from jax import lax
from jax.sharding import PartitionSpec as P


def causal_probs(query_heads, key_rows):
    head_size = key_rows.shape[-1]
    length = key_rows.shape[0]
    logits = jnp.einsum("qgd,pd->gqp", query_heads, key_rows, preferred_element_type=jnp.float32)
    logits = logits * (1.0 / math.sqrt(head_size))
    row_pos = lax.broadcasted_iota(jnp.int32, (length, length), 0)
    col_pos = lax.broadcasted_iota(jnp.int32, (length, length), 1)
    logits = jnp.where(col_pos <= row_pos, logits, -jnp.inf)
    return jax.nn.softmax(logits, axis=-1).astype(jnp.bfloat16)


def shift(value, axis, by):
    length = lax.axis_size(axis)
    return lax.ppermute(value, axis, [(i, (i + by) % length) for i in range(length)])


def blocks_of_all(value):
    copies = jnp.broadcast_to(value[None], (lax.axis_size("tensor"),) + value.shape)
    return lax.all_to_all(copies, "tensor", 0, 0)


def side_by_side(blocks):
    count, rows, columns = blocks.shape
    return blocks.transpose(1, 0, 2).reshape(rows, count * columns)


def gather_rows(value):
    count = lax.axis_size("tensor")
    me = lax.axis_index("tensor")
    out = jnp.zeros((count,) + value.shape, value.dtype)
    out = lax.dynamic_update_index_in_dim(out, value, me, 0)
    for by in range(1, count):
        got = shift(value, "tensor", by)
        out = lax.dynamic_update_index_in_dim(out, got, (me - by) % count, 0)
    return out.reshape(count * value.shape[0], value.shape[1])


def on_device(grad_top, query, keys, values, out_weight, value_weight):
    sections = lax.axis_size("section")
    place = lax.axis_index("section")
    me = lax.axis_index("tensor")
    micro_batch, length = query.shape[1], query.shape[2]
    rows = micro_batch * length
    head_size = keys.shape[3]
    group = query.shape[3] // head_size
    feat_local = grad_top.shape[2]
    query_heads = query[0].reshape(micro_batch, length, group, head_size)
    probs = jax.vmap(causal_probs)(query_heads, keys[0])
    mixed = jnp.einsum("mgqp,mpd->mqgd", probs, values[0], preferred_element_type=jnp.float32)
    mixed = mixed.astype(jnp.bfloat16).reshape(rows, group * head_size)
    out_mat = out_weight[0]
    value_full = gather_rows(shift(value_weight[0], "section", -1))
    incoming = side_by_side(blocks_of_all(grad_top.reshape(rows, feat_local)))
    saved = incoming
    for turn in range(sections):
        if turn:
            saved = jnp.where(turn == sections - 1 - place, incoming, saved)
        attn_grad = lax.dot_general(
            incoming, out_mat, (((1,), (1,)), ((), ())), preferred_element_type=jnp.float32
        )
        attn_grad = attn_grad.astype(jnp.bfloat16).reshape(micro_batch, length, group, head_size)
        value_grad = jnp.einsum(
            "mgqp,mqgd->mpd", probs, attn_grad, preferred_element_type=jnp.float32
        ).astype(jnp.bfloat16)
        moved = shift(value_grad.reshape(rows, head_size), "section", -1)
        incoming = shift(incoming, "section", -1)
        every_head = side_by_side(blocks_of_all(moved))
        branch = lax.dot_general(
            every_head, value_full, (((1,), (1,)), ((), ())), preferred_element_type=jnp.float32
        )
        incoming = (incoming.astype(jnp.float32) + branch).astype(jnp.bfloat16)
    weight_grad = lax.dot_general(
        mixed, saved, (((0,), (0,)), ((), ())), preferred_element_type=jnp.float32
    ).astype(jnp.bfloat16)
    final = jnp.where(place == sections - 1, incoming, saved)
    grads = shift(lax.dynamic_slice_in_dim(final, me * feat_local, feat_local, 1), "section", 1)
    return (grads.reshape(1, micro_batch, length, feat_local), weight_grad[None])


def solution(mesh):
    placed = (
        P(None, None, "tensor"),
        P("section", None, None, "tensor"),
        P("section", None, None, "tensor"),
        P("section", None, None, "tensor"),
        P("section", "tensor", None),
        P("section", "tensor", None),
    )
    return jax.shard_map(
        on_device,
        mesh=mesh,
        in_specs=placed,
        out_specs=(P("section", None, None, "tensor"), P("section", "tensor", None)),
        check_vma=False,
    )
```

```python
import functools
import math

import jax
import jax.numpy as jnp
from jax import lax
from jax.experimental import pallas as pl
from jax.experimental.pallas import tpu as pltpu
from jax.sharding import PartitionSpec as P

F32 = jnp.float32
BF16 = jnp.bfloat16
NN = (((1,), (0,)), ((), ()))
TN = (((0,), (0,)), ((), ()))


def causal_probs(query_heads, key_rows):
    head_size = key_rows.shape[-1]
    length = key_rows.shape[0]
    logits = jnp.einsum("qgd,pd->gqp", query_heads, key_rows, preferred_element_type=F32)
    logits = logits * (1.0 / math.sqrt(head_size))
    row_pos = lax.broadcasted_iota(jnp.int32, (length, length), 0)
    col_pos = lax.broadcasted_iota(jnp.int32, (length, length), 1)
    logits = jnp.where(col_pos <= row_pos, logits, -jnp.inf)
    return jax.nn.softmax(logits, axis=-1).astype(BF16)


def shift(value, axis, by):
    length = lax.axis_size(axis)
    return lax.ppermute(value, axis, [(i, (i + by) % length) for i in range(length)])


def blocks_of_all(value):
    copies = jnp.broadcast_to(value[None], (lax.axis_size("tensor"),) + value.shape)
    return lax.all_to_all(copies, "tensor", 0, 0)


def value_grad_of(total, probs_t_ref, value_ref):
    attn = total.astype(BF16)
    micro_batch, length, depth = probs_t_ref.shape
    head_size = value_ref.shape[1]
    for m in range(micro_batch):
        rows = slice(m * length, (m + 1) * length)
        heads = [
            attn[rows, g * head_size : (g + 1) * head_size] for g in range(depth // length)
        ]
        value_ref[rows, :] = lax.dot_general(
            probs_t_ref[m], jnp.concatenate(heads, 0), NN, preferred_element_type=F32
        ).astype(BF16)


def first_kernel(steps, rows_ref, weight_ref, probs_t_ref, value_ref, total):
    step = pl.program_id(0)

    @pl.when(step == 0)
    def _():
        total[...] = jnp.zeros_like(total)

    total[...] += lax.dot_general(rows_ref[...], weight_ref[...], NN, preferred_element_type=F32)

    @pl.when(step == steps - 1)
    def _():
        value_grad_of(total[...], probs_t_ref, value_ref)


def turn_kernel(
    steps, flag_ref, blocks_ref, rows_ref, back_ref, weight_ref, probs_t_ref, kept_ref,
    new_ref, value_ref, saved_ref, heads, total, sem,
):
    step = pl.program_id(0)
    head_size = blocks_ref.shape[2]

    @pl.when(step == 0)
    def _():
        for c in range(blocks_ref.shape[0]):
            heads[:, c * head_size : (c + 1) * head_size] = blocks_ref[c]
        total[...] = jnp.zeros_like(total)

    branch = lax.dot_general(heads[...], back_ref[0], NN, preferred_element_type=F32)
    new_rows = (rows_ref[...].astype(F32) + branch).astype(BF16)
    new_ref[...] = new_rows
    total[...] += lax.dot_general(new_rows, weight_ref[...], NN, preferred_element_type=F32)

    @pl.when(flag_ref[0] == 1)
    def _():
        width = new_ref.shape[1]
        spot = pl.ds(pl.multiple_of(step * width, width), width)
        copy = pltpu.make_async_copy(new_ref, saved_ref.at[:, spot], sem)
        copy.start()
        copy.wait()

    @pl.when(step == steps - 1)
    def _():
        value_grad_of(total[...], probs_t_ref, value_ref)


def first_value_grad(rows, weight_t, probs_t):
    count, width = rows.shape
    own = weight_t.shape[1]
    steps = 4
    tile = width // steps
    head_size = 128
    return pl.pallas_call(
        functools.partial(first_kernel, steps),
        grid=(steps,),
        in_specs=[
            pl.BlockSpec((count, tile), lambda i: (0, i)),
            pl.BlockSpec((tile, own), lambda i: (i, 0)),
            pl.BlockSpec(probs_t.shape, lambda i: (0, 0, 0)),
        ],
        out_specs=pl.BlockSpec((count, head_size), lambda i: (0, 0)),
        out_shape=jax.ShapeDtypeStruct((count, head_size), BF16),
        scratch_shapes=[pltpu.VMEM((count, own), F32)],
        compiler_params=pltpu.CompilerParams(vmem_limit_bytes=24 << 20),
        cost_estimate=pl.CostEstimate(
            flops=2 * count * width * own, bytes_accessed=2 * width * own, transcendentals=0
        ),
        name="first_turn",
    )(rows, weight_t, probs_t)


def turn(flag, blocks, rows, back, weight_t, probs_t, saved):
    count, width = rows.shape
    own = weight_t.shape[1]
    steps, depth, tile = back.shape
    head_size = blocks.shape[2]
    return pl.pallas_call(
        functools.partial(turn_kernel, steps),
        grid=(steps,),
        in_specs=[
            pl.BlockSpec(memory_space=pltpu.SMEM),
            pl.BlockSpec(blocks.shape, lambda i: (0, 0, 0)),
            pl.BlockSpec((count, tile), lambda i: (0, i)),
            pl.BlockSpec((1, depth, tile), lambda i: (i, 0, 0)),
            pl.BlockSpec((tile, own), lambda i: (i, 0)),
            pl.BlockSpec(probs_t.shape, lambda i: (0, 0, 0)),
            pl.BlockSpec(memory_space=pl.ANY),
        ],
        out_specs=[
            pl.BlockSpec((count, tile), lambda i: (0, i)),
            pl.BlockSpec((count, head_size), lambda i: (0, 0)),
            pl.BlockSpec(memory_space=pl.ANY),
        ],
        out_shape=[
            jax.ShapeDtypeStruct(rows.shape, BF16),
            jax.ShapeDtypeStruct((count, head_size), BF16),
            jax.ShapeDtypeStruct(rows.shape, BF16),
        ],
        scratch_shapes=[
            pltpu.VMEM((count, depth), BF16),
            pltpu.VMEM((count, own), F32),
            pltpu.SemaphoreType.DMA,
        ],
        input_output_aliases={6: 2},
        compiler_params=pltpu.CompilerParams(vmem_limit_bytes=24 << 20),
        cost_estimate=pl.CostEstimate(
            flops=2 * count * width * (own + depth),
            bytes_accessed=2 * width * (own + depth),
            transcendentals=0,
        ),
        name="turn",
    )(flag, blocks, rows, back, weight_t, probs_t, saved)


def on_device(grad_top, query, keys, values, out_weight, value_weight):
    sections = lax.axis_size("section")
    place = lax.axis_index("section")
    me = lax.axis_index("tensor")
    micro_batch, length = query.shape[1], query.shape[2]
    rows = micro_batch * length
    head_size = keys.shape[3]
    group = query.shape[3] // head_size
    feat_local = grad_top.shape[2]
    back = lax.all_gather(shift(value_weight[0].T, "section", -1), "tensor", axis=0)
    top = blocks_of_all(grad_top.reshape(rows, feat_local))
    incoming = top.transpose(1, 0, 2).reshape(rows, top.shape[0] * feat_local)
    query_heads = query[0].reshape(micro_batch, length, group, head_size)
    probs = jax.vmap(causal_probs)(query_heads, keys[0])
    mixed = jnp.einsum("mgqp,mpd->mqgd", probs, values[0], preferred_element_type=F32)
    mixed = mixed.astype(BF16).reshape(rows, group * head_size)
    probs_t = probs.transpose(0, 3, 1, 2).reshape(micro_batch, length, group * length)
    weight_t = out_weight[0].T
    saved = incoming
    value_grad = first_value_grad(incoming, weight_t, probs_t)
    for number in range(1, sections + 1):
        moved = shift(value_grad, "section", -1)
        incoming, moved = lax.optimization_barrier((incoming, moved))
        incoming = shift(incoming, "section", -1)
        blocks = blocks_of_all(moved)
        if number < sections:
            flag = (place == sections - 1 - number).astype(jnp.int32).reshape(1)
            incoming, value_grad, saved = turn(
                flag, blocks, incoming, back, weight_t, probs_t, saved
            )
    heads = blocks.transpose(1, 0, 2).reshape(rows, blocks.shape[0] * head_size)
    own = lax.dynamic_slice_in_dim(incoming, me * feat_local, feat_local, 1)
    branch = jnp.dot(
        heads, lax.dynamic_index_in_dim(back, me, 0, keepdims=False), preferred_element_type=F32
    )
    last = (own.astype(F32) + branch).astype(BF16)
    weight_grad = lax.dot_general(mixed, saved, TN, preferred_element_type=F32).astype(BF16)
    own = lax.dynamic_slice_in_dim(saved, me * feat_local, feat_local, 1)
    grads = shift(jnp.where(place == sections - 1, last, own), "section", 1)
    return (grads.reshape(1, micro_batch, length, feat_local), weight_grad[None])


def solution(mesh):
    placed = (
        P(None, None, "tensor"),
        P("section", None, None, "tensor"),
        P("section", None, None, "tensor"),
        P("section", None, None, "tensor"),
        P("section", "tensor", None),
        P("section", "tensor", None),
    )
    return jax.shard_map(
        on_device,
        mesh=mesh,
        in_specs=placed,
        out_specs=(P("section", None, None, "tensor"), P("section", "tensor", None)),
        check_vma=False,
    )
```

```python
import functools
import math

import jax
import jax.numpy as jnp
from jax import lax
from jax.experimental import pallas as pl
from jax.experimental.pallas import tpu as pltpu
from jax.sharding import PartitionSpec as P

F32 = jnp.float32
BF16 = jnp.bfloat16
NN = (((1,), (0,)), ((), ()))
NT = (((1,), (1,)), ((), ()))
TN = (((0,), (0,)), ((), ()))


def causal_probs(query_heads, key_rows):
    head_size = key_rows.shape[-1]
    length = key_rows.shape[0]
    logits = jnp.einsum("qgd,pd->gqp", query_heads, key_rows, preferred_element_type=F32)
    logits = logits * (1.0 / math.sqrt(head_size))
    row_pos = lax.broadcasted_iota(jnp.int32, (length, length), 0)
    col_pos = lax.broadcasted_iota(jnp.int32, (length, length), 1)
    logits = jnp.where(col_pos <= row_pos, logits, -jnp.inf)
    return jax.nn.softmax(logits, axis=-1).astype(BF16)


def shift(value, axis, by):
    length = lax.axis_size(axis)
    return lax.ppermute(value, axis, [(i, (i + by) % length) for i in range(length)])


def hand_down(value, section):
    length = lax.axis_size("section")
    half = length // 2
    if section % 2:
        pairs = [(i, i ^ 1) for i in range(length)]
    else:
        lows = [section - 1] if section == half else [
            i for i in range(1, length - 1, 2) if i != half - 1
        ]
        other = {i: i for i in range(length)}
        for low in lows:
            other[low], other[low + 1] = low + 1, low
        pairs = sorted(other.items())
    return lax.ppermute(value, "section", pairs)


def copies_kernel(value_ref, out_ref):
    for c in range(out_ref.shape[0]):
        out_ref[c] = value_ref[...]


def blocks_of_all(value):
    shape = (lax.axis_size("tensor"),) + value.shape
    copies = pl.pallas_call(
        copies_kernel,
        in_specs=[pl.BlockSpec(memory_space=pltpu.VMEM)],
        out_specs=pl.BlockSpec(memory_space=pltpu.VMEM),
        out_shape=jax.ShapeDtypeStruct(shape, value.dtype),
        compiler_params=pltpu.CompilerParams(vmem_limit_bytes=6 << 20),
        cost_estimate=pl.CostEstimate(
            flops=0, bytes_accessed=2 * math.prod(shape), transcendentals=0
        ),
        name="copies",
    )(value)
    return lax.all_to_all(copies, "tensor", 0, 0)


def transpose_kernel(value_ref, out_ref):
    out_ref[...] = value_ref[...].T


def transposed(value, tile=512):
    rows, columns = value.shape
    return pl.pallas_call(
        transpose_kernel,
        grid=(columns // tile,),
        in_specs=[pl.BlockSpec((rows, tile), lambda i: (0, i))],
        out_specs=pl.BlockSpec((tile, rows), lambda i: (i, 0)),
        out_shape=jax.ShapeDtypeStruct((columns, rows), value.dtype),
        compiler_params=pltpu.CompilerParams(vmem_limit_bytes=12 << 20),
        cost_estimate=pl.CostEstimate(
            flops=0, bytes_accessed=4 * rows * columns, transcendentals=0
        ),
        name="transposed",
    )(value)


def value_grad_of(total, probs_t_ref, value_ref):
    attn = total.astype(BF16)
    micro_batch, length, depth = probs_t_ref.shape
    head_size = value_ref.shape[1]
    for m in range(micro_batch):
        rows = slice(m * length, (m + 1) * length)
        heads = [
            attn[rows, g * head_size : (g + 1) * head_size] for g in range(depth // length)
        ]
        value_ref[rows, :] = lax.dot_general(
            probs_t_ref[m], jnp.concatenate(heads, 0), NN, preferred_element_type=F32
        ).astype(BF16)


def first_kernel(steps, rows_ref, weight_ref, probs_t_ref, value_ref, total):
    step = pl.program_id(0)

    @pl.when(step == 0)
    def _():
        total[...] = jnp.zeros_like(total)

    total[...] += lax.dot_general(rows_ref[...], weight_ref[...], NN, preferred_element_type=F32)

    @pl.when(step == steps - 1)
    def _():
        value_grad_of(total[...], probs_t_ref, value_ref)


def turn_kernel(
    steps, section, place_ref, blocks_ref, rows_ref, back_ref, weight_ref, probs_t_ref, kept_ref,
    new_ref, value_ref, saved_ref, heads, total, sem,
):
    step = pl.program_id(0)
    head_size = blocks_ref.shape[2]

    @pl.when(step == 0)
    def _():
        for c in range(blocks_ref.shape[0]):
            heads[:, c * head_size : (c + 1) * head_size] = blocks_ref[c]
        total[...] = jnp.zeros_like(total)

    branch = lax.dot_general(heads[...], back_ref[0], NN, preferred_element_type=F32)
    new_rows = (rows_ref[...].astype(F32) + branch).astype(BF16)
    new_ref[...] = new_rows
    total[...] += lax.dot_general(new_rows, weight_ref[...], NN, preferred_element_type=F32)

    @pl.when(place_ref[0] == section)
    def _():
        width = new_ref.shape[1]
        spot = pl.ds(pl.multiple_of(step * width, width), width)
        copy = pltpu.make_async_copy(new_ref, saved_ref.at[:, spot], sem)
        copy.start()
        copy.wait()

    @pl.when(step == steps - 1)
    def _():
        value_grad_of(total[...], probs_t_ref, value_ref)


def first_value_grad(rows, weight_t, probs_t):
    count, width = rows.shape
    own = weight_t.shape[1]
    steps = 4
    tile = width // steps
    head_size = 128
    return pl.pallas_call(
        functools.partial(first_kernel, steps),
        grid=(steps,),
        in_specs=[
            pl.BlockSpec((count, tile), lambda i: (0, i)),
            pl.BlockSpec((tile, own), lambda i: (i, 0)),
            pl.BlockSpec(probs_t.shape, lambda i: (0, 0, 0)),
        ],
        out_specs=pl.BlockSpec((count, head_size), lambda i: (0, 0)),
        out_shape=jax.ShapeDtypeStruct((count, head_size), BF16),
        scratch_shapes=[pltpu.VMEM((count, own), F32)],
        compiler_params=pltpu.CompilerParams(vmem_limit_bytes=16 << 20),
        cost_estimate=pl.CostEstimate(
            flops=2 * count * width * own, bytes_accessed=2 * width * own, transcendentals=0
        ),
        name="first_turn",
    )(rows, weight_t, probs_t)


def turn(section, place, blocks, rows, back, weight_t, probs_t, saved):
    count, width = rows.shape
    own = weight_t.shape[1]
    steps, depth, tile = back.shape
    head_size = blocks.shape[2]
    return pl.pallas_call(
        functools.partial(turn_kernel, steps, section),
        grid=(steps,),
        in_specs=[
            pl.BlockSpec(memory_space=pltpu.SMEM),
            pl.BlockSpec(blocks.shape, lambda i: (0, 0, 0)),
            pl.BlockSpec((count, tile), lambda i: (0, i)),
            pl.BlockSpec((1, depth, tile), lambda i: (i, 0, 0)),
            pl.BlockSpec((tile, own), lambda i: (i, 0)),
            pl.BlockSpec(probs_t.shape, lambda i: (0, 0, 0)),
            pl.BlockSpec(memory_space=pl.ANY),
        ],
        out_specs=[
            pl.BlockSpec((count, tile), lambda i: (0, i)),
            pl.BlockSpec((count, head_size), lambda i: (0, 0)),
            pl.BlockSpec(memory_space=pl.ANY),
        ],
        out_shape=[
            jax.ShapeDtypeStruct(rows.shape, BF16),
            jax.ShapeDtypeStruct((count, head_size), BF16),
            jax.ShapeDtypeStruct(rows.shape, BF16),
        ],
        scratch_shapes=[
            pltpu.VMEM((count, depth), BF16),
            pltpu.VMEM((count, own), F32),
            pltpu.SemaphoreType.DMA,
        ],
        input_output_aliases={6: 2},
        compiler_params=pltpu.CompilerParams(vmem_limit_bytes=16 << 20),
        cost_estimate=pl.CostEstimate(
            flops=2 * count * width * (own + depth),
            bytes_accessed=2 * width * (own + depth),
            transcendentals=0,
        ),
        name="turn",
    )(place, blocks, rows, back, weight_t, probs_t, saved)


def on_device(grad_top, query, keys, values, out_weight, value_weight):
    sections = lax.axis_size("section")
    place = lax.axis_index("section")
    me = lax.axis_index("tensor")
    micro_batch, length = query.shape[1], query.shape[2]
    rows = micro_batch * length
    head_size = keys.shape[3]
    group = query.shape[3] // head_size
    feat_local = grad_top.shape[2]
    back = lax.all_gather(shift(transposed(value_weight[0]), "section", -1), "tensor", axis=0)
    top = blocks_of_all(grad_top.reshape(rows, feat_local))
    incoming = top.transpose(1, 0, 2).reshape(rows, top.shape[0] * feat_local)
    query_heads = query[0].reshape(micro_batch, length, group, head_size)
    probs = jax.vmap(causal_probs)(query_heads, keys[0])
    mixed = jnp.einsum("mgqp,mpd->mqgd", probs, values[0], preferred_element_type=F32)
    mixed = mixed.astype(BF16).reshape(rows, group * head_size)
    probs_t = probs.transpose(0, 3, 1, 2).reshape(micro_batch, length, group * length)
    weight_t = transposed(out_weight[0])
    spot = place.astype(jnp.int32).reshape(1)
    saved = incoming
    value_grad = first_value_grad(incoming, weight_t, probs_t)
    for section in range(sections - 1, 0, -1):
        moved = hand_down(value_grad, section)
        incoming, moved = lax.optimization_barrier((incoming, moved))
        incoming = hand_down(incoming, section)
        blocks = blocks_of_all(moved)
        incoming, value_grad, saved = turn(
            section - 1, spot, blocks, incoming, back, weight_t, probs_t, saved
        )
    own = lax.dynamic_slice_in_dim(saved, me * feat_local, feat_local, 1)
    above = shift(own, "section", 1)
    blocks = blocks_of_all(value_grad)
    weight_grad = lax.dot_general(mixed, saved, TN, preferred_element_type=F32).astype(BF16)
    heads = blocks.transpose(1, 0, 2).reshape(rows, blocks.shape[0] * head_size)
    branch = lax.dot_general(heads, value_weight[0], NT, preferred_element_type=F32)
    last = (own.astype(F32) + branch).astype(BF16)
    grads = jnp.where(place == 0, last, above)
    return (grads.reshape(1, micro_batch, length, feat_local), weight_grad[None])


def solution(mesh):
    placed = (
        P(None, None, "tensor"),
        P("section", None, None, "tensor"),
        P("section", None, None, "tensor"),
        P("section", None, None, "tensor"),
        P("section", "tensor", None),
        P("section", "tensor", None),
    )
    return jax.shard_map(
        on_device,
        mesh=mesh,
        in_specs=placed,
        out_specs=(P("section", None, None, "tensor"), P("section", "tensor", None)),
        check_vma=False,
    )
```

```python
import functools
import math

import jax
import jax.numpy as jnp
from jax import lax
from jax.experimental import pallas as pl
from jax.experimental.pallas import tpu as pltpu
from jax.sharding import PartitionSpec as P

F32 = jnp.float32
BF16 = jnp.bfloat16
NN = (((1,), (0,)), ((), ()))


def causal_probs(query_heads, key_rows):
    head_size = key_rows.shape[-1]
    length = key_rows.shape[0]
    logits = jnp.einsum("qgd,pd->gqp", query_heads, key_rows, preferred_element_type=F32)
    logits = logits * (1.0 / math.sqrt(head_size))
    row_pos = lax.broadcasted_iota(jnp.int32, (length, length), 0)
    col_pos = lax.broadcasted_iota(jnp.int32, (length, length), 1)
    logits = jnp.where(col_pos <= row_pos, logits, -jnp.inf)
    return jax.nn.softmax(logits, axis=-1).astype(BF16)


def shift(value, axis, by):
    length = lax.axis_size(axis)
    return lax.ppermute(value, axis, [(i, (i + by) % length) for i in range(length)])


def hand_down(value, section):
    length = lax.axis_size("section")
    half = length // 2
    if section % 2:
        pairs = [(i, i ^ 1) for i in range(length)]
    else:
        lows = [section - 1] if section == half else [
            i for i in range(1, length - 1, 2) if i != half - 1
        ]
        other = {i: i for i in range(length)}
        for low in lows:
            other[low], other[low + 1] = low + 1, low
        pairs = sorted(other.items())
    return lax.ppermute(value, "section", pairs)


def copies_kernel(value_ref, out_ref):
    for c in range(out_ref.shape[0]):
        out_ref[c] = value_ref[...]


def blocks_of_all(value):
    shape = (lax.axis_size("tensor"),) + value.shape
    copies = pl.pallas_call(
        copies_kernel,
        in_specs=[pl.BlockSpec(memory_space=pltpu.VMEM)],
        out_specs=pl.BlockSpec(memory_space=pltpu.VMEM),
        out_shape=jax.ShapeDtypeStruct(shape, value.dtype),
        compiler_params=pltpu.CompilerParams(vmem_limit_bytes=6 << 20),
        cost_estimate=pl.CostEstimate(
            flops=0, bytes_accessed=2 * math.prod(shape), transcendentals=0
        ),
        name="copies",
    )(value)
    return lax.all_to_all(copies, "tensor", 0, 0)


def transpose_kernel(value_ref, out_ref):
    out_ref[...] = value_ref[...].T


def transposed(value, tile=512, first=0, count=None):
    rows, columns = value.shape
    count = columns // tile if count is None else count
    return pl.pallas_call(
        transpose_kernel,
        grid=(count,),
        in_specs=[pl.BlockSpec((rows, tile), lambda i: (0, i + first))],
        out_specs=pl.BlockSpec((tile, rows), lambda i: (i, 0)),
        out_shape=jax.ShapeDtypeStruct((count * tile, rows), value.dtype),
        compiler_params=pltpu.CompilerParams(vmem_limit_bytes=12 << 20),
        cost_estimate=pl.CostEstimate(
            flops=0, bytes_accessed=4 * rows * count * tile, transcendentals=0
        ),
        name="transposed",
    )(value)


def place_kernel(spots, given, index_ref, *refs):
    pieces, out_ref, sems = refs[:given], refs[-2], refs[-1]
    copies = []
    for i, (piece, (slot, row)) in enumerate(zip(pieces, spots)):
        goal = out_ref.at[index_ref[slot], pl.ds(row, piece.shape[0])]
        copies.append(pltpu.make_async_copy(piece, goal, sems.at[i]))
    for copy in copies:
        copy.start()
    for copy in copies:
        copy.wait()


def put(index, pieces, shape, whole=None):
    arrays = [piece[0] for piece in pieces]
    spots = [piece[1:] for piece in pieces]
    more = [] if whole is None else [whole]
    return pl.pallas_call(
        functools.partial(place_kernel, spots, len(arrays)),
        in_specs=[pl.BlockSpec(memory_space=pltpu.SMEM)]
        + [pl.BlockSpec(memory_space=pl.ANY)] * (len(arrays) + len(more)),
        out_specs=pl.BlockSpec(memory_space=pl.ANY),
        out_shape=jax.ShapeDtypeStruct(shape, arrays[0].dtype),
        scratch_shapes=[pltpu.SemaphoreType.DMA((len(arrays),))],
        input_output_aliases={1 + len(arrays): 0} if more else {},
        compiler_params=pltpu.CompilerParams(vmem_limit_bytes=1 << 20),
        cost_estimate=pl.CostEstimate(
            flops=0,
            bytes_accessed=4 * sum(math.prod(array.shape) for array in arrays),
            transcendentals=0,
        ),
        name="put",
    )(index, *arrays, *more)


def across(value, x_by=0, z_by=0):
    length = lax.axis_size("tensor")
    xs = length // 2
    pairs = []
    for i in range(length):
        z, x = divmod(i, xs)
        pairs.append((i, (z + z_by) % 2 * xs + (x + x_by) % xs))
    return lax.ppermute(value, "tensor", pairs)


def gather_back(index, whole, halves, beside):
    n, k = whole.shape
    half = n // 2
    low, high = halves
    other = across(whole, 0, 1)
    left_low, right_low = across(low, 1), across(low, -1)
    left_high, right_high = across(high, 1), across(high, -1)
    first = (other, left_low, right_low, left_high, right_high)
    first, beside = lax.optimization_barrier((first, beside))
    other, left_low, right_low, left_high, right_high = first
    cross_left, cross_right = across(left_high, 0, 1), across(right_high, 0, 1)
    far_high, far_low = across(right_high, -1), across(left_low, 1)
    next_left, next_right = across(other[:half], 1), across(other[:half], -1)
    early = [
        (whole, 0, 0), (left_low, 1, 0), (left_high, 1, half),
        (right_low, 2, 0), (right_high, 2, half), (other, 4, 0),
    ]
    late = [
        (far_low, 3, 0), (far_high, 3, half),
        (next_left, 5, 0), (cross_left, 5, half), (next_right, 6, 0), (cross_right, 6, half),
        (across(next_left, 1), 7, 0), (across(far_high, 0, 1), 7, half),
    ]
    shape = (lax.axis_size("tensor"), n, k)
    whole, far_high = lax.optimization_barrier((whole, far_high))
    early[0], late[1] = (whole, 0, 0), (far_high, 3, half)
    return put(index, late, shape, put(index, early, shape)), beside


def value_grad_of(total, probs_t_ref, value_ref):
    attn = total.astype(BF16)
    micro_batch, length, depth = probs_t_ref.shape
    head_size = value_ref.shape[1]
    for m in range(micro_batch):
        rows = slice(m * length, (m + 1) * length)
        heads = [
            attn[rows, g * head_size : (g + 1) * head_size] for g in range(depth // length)
        ]
        value_ref[rows, :] = lax.dot_general(
            probs_t_ref[m], jnp.concatenate(heads, 0), NN, preferred_element_type=F32
        ).astype(BF16)


def keep(step, block, saved_ref, sem):
    copy = pltpu.make_async_copy(block, saved_ref.at[step], sem)
    copy.start()
    copy.wait()


def plain_kernel(
    steps, section, place_ref, rows_ref, weight_ref, probs_t_ref, kept_ref,
    value_ref, saved_ref, total, sem,
):
    step = pl.program_id(0)

    @pl.when(step == 0)
    def _():
        total[...] = jnp.zeros_like(total)

    total[...] += lax.dot_general(rows_ref[0], weight_ref[...], NN, preferred_element_type=F32)

    @pl.when(place_ref[0] == section)
    def _():
        keep(step, rows_ref.at[0], saved_ref, sem)

    @pl.when(step == steps - 1)
    def _():
        value_grad_of(total[...], probs_t_ref, value_ref)


def turn_kernel(
    steps, section, place_ref, blocks_ref, rows_ref, back_ref, weight_ref, probs_t_ref, kept_ref,
    new_ref, value_ref, saved_ref, heads, total, sem,
):
    step = pl.program_id(0)
    head_size = blocks_ref.shape[2]

    @pl.when(step == 0)
    def _():
        for c in range(blocks_ref.shape[0]):
            heads[:, c * head_size : (c + 1) * head_size] = blocks_ref[c]
        total[...] = jnp.zeros_like(total)

    branch = lax.dot_general(heads[...], back_ref[0], NN, preferred_element_type=F32)
    new_rows = (rows_ref[0].astype(F32) + branch).astype(BF16)
    new_ref[0] = new_rows
    total[...] += lax.dot_general(new_rows, weight_ref[...], NN, preferred_element_type=F32)

    @pl.when(place_ref[0] == section)
    def _():
        keep(step, new_ref.at[0], saved_ref, sem)

    @pl.when(step == steps - 1)
    def _():
        value_grad_of(total[...], probs_t_ref, value_ref)


def params():
    return pltpu.CompilerParams(vmem_limit_bytes=16 << 20)


def plain_turn(section, place, rows, weight_t, probs_t, saved):
    steps, count, tile = rows.shape
    own = weight_t.shape[1]
    head_size = 128
    return pl.pallas_call(
        functools.partial(plain_kernel, steps, section),
        grid=(steps,),
        in_specs=[
            pl.BlockSpec(memory_space=pltpu.SMEM),
            pl.BlockSpec((1, count, tile), lambda i: (i, 0, 0)),
            pl.BlockSpec((tile, own), lambda i: (i, 0)),
            pl.BlockSpec(probs_t.shape, lambda i: (0, 0, 0)),
            pl.BlockSpec(memory_space=pl.ANY),
        ],
        out_specs=[
            pl.BlockSpec((count, head_size), lambda i: (0, 0)),
            pl.BlockSpec(memory_space=pl.ANY),
        ],
        out_shape=[
            jax.ShapeDtypeStruct((count, head_size), BF16),
            jax.ShapeDtypeStruct(saved.shape, BF16),
        ],
        scratch_shapes=[pltpu.VMEM((count, own), F32), pltpu.SemaphoreType.DMA],
        input_output_aliases={4: 1},
        compiler_params=params(),
        cost_estimate=pl.CostEstimate(
            flops=2 * steps * count * tile * own,
            bytes_accessed=2 * steps * tile * own,
            transcendentals=0,
        ),
        name="plain_turn",
    )(place, rows, weight_t, probs_t, saved)


def turn(section, place, blocks, rows, back, weight_t, probs_t, saved):
    count = rows.shape[1]
    own = weight_t.shape[1]
    steps, depth, tile = back.shape
    head_size = blocks.shape[2]
    return pl.pallas_call(
        functools.partial(turn_kernel, steps, section),
        grid=(steps,),
        in_specs=[
            pl.BlockSpec(memory_space=pltpu.SMEM),
            pl.BlockSpec(blocks.shape, lambda i: (0, 0, 0)),
            pl.BlockSpec((1, count, tile), lambda i: (i, 0, 0)),
            pl.BlockSpec((1, depth, tile), lambda i: (i, 0, 0)),
            pl.BlockSpec((tile, own), lambda i: (i, 0)),
            pl.BlockSpec(probs_t.shape, lambda i: (0, 0, 0)),
            pl.BlockSpec(memory_space=pl.ANY),
        ],
        out_specs=[
            pl.BlockSpec((1, count, tile), lambda i: (i, 0, 0)),
            pl.BlockSpec((count, head_size), lambda i: (0, 0)),
            pl.BlockSpec(memory_space=pl.ANY),
        ],
        out_shape=[
            jax.ShapeDtypeStruct(rows.shape, BF16),
            jax.ShapeDtypeStruct((count, head_size), BF16),
            jax.ShapeDtypeStruct(saved.shape, BF16),
        ],
        scratch_shapes=[
            pltpu.VMEM((count, depth), BF16),
            pltpu.VMEM((count, own), F32),
            pltpu.SemaphoreType.DMA,
        ],
        input_output_aliases={6: 2},
        compiler_params=params(),
        cost_estimate=pl.CostEstimate(
            flops=2 * steps * count * tile * (own + depth),
            bytes_accessed=2 * steps * tile * (own + depth),
            transcendentals=0,
        ),
        name="turn",
    )(place, blocks, rows, back, weight_t, probs_t, saved)


def pick_kernel(me_ref, rows_ref, out_ref):
    out_ref[...] = rows_ref[0]


def pick(me, rows):
    _, count, tile = rows.shape
    return pl.pallas_call(
        pick_kernel,
        grid_spec=pltpu.PrefetchScalarGridSpec(
            num_scalar_prefetch=1,
            grid=(1,),
            in_specs=[pl.BlockSpec((1, count, tile), lambda i, me: (me[0], 0, 0))],
            out_specs=pl.BlockSpec((count, tile), lambda i, me: (0, 0)),
        ),
        out_shape=jax.ShapeDtypeStruct((count, tile), rows.dtype),
        compiler_params=pltpu.CompilerParams(vmem_limit_bytes=4 << 20),
        name="pick",
    )(me, rows)


def last_kernel(place_ref, me_ref, blocks_ref, rows_ref, value_t_ref, above_ref, out_ref, heads):
    head_size = blocks_ref.shape[2]

    @pl.when(place_ref[0] == 0)
    def _():
        for c in range(blocks_ref.shape[0]):
            heads[:, c * head_size : (c + 1) * head_size] = blocks_ref[c]
        branch = lax.dot_general(heads[...], value_t_ref[...], NN, preferred_element_type=F32)
        out_ref[...] = (rows_ref[0].astype(F32) + branch).astype(BF16)

    @pl.when(place_ref[0] != 0)
    def _():
        out_ref[...] = above_ref[...]


def last_features(place, me, blocks, rows, value_t, above):
    _, count, tile = rows.shape
    depth = value_t.shape[0]
    return pl.pallas_call(
        last_kernel,
        grid_spec=pltpu.PrefetchScalarGridSpec(
            num_scalar_prefetch=2,
            grid=(1,),
            in_specs=[
                pl.BlockSpec(blocks.shape, lambda i, place, me: (0, 0, 0)),
                pl.BlockSpec((1, count, tile), lambda i, place, me: (me[0], 0, 0)),
                pl.BlockSpec(value_t.shape, lambda i, place, me: (0, 0)),
                pl.BlockSpec((count, tile), lambda i, place, me: (0, 0)),
            ],
            out_specs=pl.BlockSpec((count, tile), lambda i, place, me: (0, 0)),
            scratch_shapes=[pltpu.VMEM((count, depth), BF16)],
        ),
        out_shape=jax.ShapeDtypeStruct((count, tile), BF16),
        compiler_params=params(),
        cost_estimate=pl.CostEstimate(
            flops=2 * count * tile * depth, bytes_accessed=2 * tile * depth, transcendentals=0
        ),
        name="last_features",
    )(place, me, blocks, rows, value_t, above)


def weight_kernel(mixed_t_ref, rows_ref, out_ref):
    out_ref[...] = lax.dot_general(
        mixed_t_ref[...], rows_ref[0], NN, preferred_element_type=F32
    ).astype(BF16)


def weight_grads(mixed_t, rows):
    steps, count, tile = rows.shape
    own = mixed_t.shape[0]
    return pl.pallas_call(
        weight_kernel,
        grid=(steps,),
        in_specs=[
            pl.BlockSpec((own, count), lambda i: (0, 0)),
            pl.BlockSpec((1, count, tile), lambda i: (i, 0, 0)),
        ],
        out_specs=pl.BlockSpec((own, tile), lambda i: (0, i)),
        out_shape=jax.ShapeDtypeStruct((own, steps * tile), BF16),
        compiler_params=params(),
        cost_estimate=pl.CostEstimate(
            flops=2 * steps * count * tile * own,
            bytes_accessed=2 * steps * tile * own,
            transcendentals=0,
        ),
        name="weight_grads",
    )(mixed_t, rows)


def on_device(grad_top, query, keys, values, out_weight, value_weight):
    sections = lax.axis_size("section")
    place = lax.axis_index("section")
    me = lax.axis_index("tensor")
    micro_batch, length = query.shape[1], query.shape[2]
    rows = micro_batch * length
    head_size = keys.shape[3]
    group = query.shape[3] // head_size
    feat_local = grad_top.shape[2]
    spot = place.astype(jnp.int32).reshape(1)
    mine = me.astype(jnp.int32).reshape(1)
    xs = lax.axis_size("tensor") // 2
    z, x = me // xs, me % xs
    index = jnp.stack(
        [
            (z + dz) % 2 * xs + (x + dx) % xs
            for dz in (0, 1)
            for dx in (0, -1, 1, 2)
        ]
    ).astype(jnp.int32)
    value_t = transposed(value_weight[0])
    top, value_t = lax.optimization_barrier((grad_top.reshape(rows, feat_local), value_t))
    whole = lax.ppermute(value_t, "section", [(i, i - 1) for i in range(1, sections)])
    incoming = blocks_of_all(top)
    query_heads = query[0].reshape(micro_batch, length, group, head_size)
    probs = jax.vmap(causal_probs)(query_heads, keys[0])
    mixed = jnp.einsum("mgqp,mpd->mqgd", probs, values[0], preferred_element_type=F32)
    mixed_t = transposed(mixed.astype(BF16).reshape(rows, group * head_size), group * head_size)
    probs_t = probs.transpose(0, 3, 1, 2).reshape(micro_batch, length, group * length)
    weight_t = transposed(out_weight[0])
    half = whole.shape[0] // 2
    whole, incoming, index, spot, mine = lax.optimization_barrier(
        (whole, incoming, index, spot, mine)
    )
    halves = lax.optimization_barrier((whole[:half], whole[half:]))
    value_grad, saved = plain_turn(
        sections - 1, spot, incoming, weight_t, probs_t, jnp.zeros_like(incoming)
    )
    beside = (incoming, value_grad, saved, mixed_t, probs_t, weight_t, value_t)
    back, beside = gather_back(index, whole, halves, beside)
    incoming, value_grad, saved, mixed_t, probs_t, weight_t, value_t = beside
    back, value_grad = lax.optimization_barrier((back, value_grad))
    for section in range(sections - 1, 0, -1):
        moved = hand_down(value_grad, section)
        incoming, moved = lax.optimization_barrier((incoming, moved))
        incoming = hand_down(incoming, section)
        blocks = blocks_of_all(moved)
        incoming, value_grad, saved = turn(
            section - 1, spot, blocks, incoming, back, weight_t, probs_t, saved
        )
    above = shift(pick(mine, saved), "section", 1)
    grads = last_features(spot, mine, blocks_of_all(value_grad), saved, value_t, above)
    return (
        grads.reshape(1, micro_batch, length, feat_local),
        weight_grads(mixed_t, saved)[None],
    )


def solution(mesh):
    placed = (
        P(None, None, "tensor"),
        P("section", None, None, "tensor"),
        P("section", None, None, "tensor"),
        P("section", None, None, "tensor"),
        P("section", "tensor", None),
        P("section", "tensor", None),
    )
    return jax.shard_map(
        on_device,
        mesh=mesh,
        in_specs=placed,
        out_specs=(P("section", None, None, "tensor"), P("section", "tensor", None)),
        check_vma=False,
    )
```

```python
import functools
import math

import jax
import jax.numpy as jnp
from jax import lax
from jax.experimental import pallas as pl
from jax.experimental.pallas import tpu as pltpu
from jax.sharding import PartitionSpec as P

F32 = jnp.float32
BF16 = jnp.bfloat16
NN = (((1,), (0,)), ((), ()))


AHEAD = 5


def causal_probs(query_heads, key_rows):
    head_size = key_rows.shape[-1]
    length = key_rows.shape[0]
    logits = jnp.einsum("qgd,pd->gqp", query_heads, key_rows, preferred_element_type=F32)
    logits = logits * (1.0 / math.sqrt(head_size))
    row_pos = lax.broadcasted_iota(jnp.int32, (length, length), 0)
    col_pos = lax.broadcasted_iota(jnp.int32, (length, length), 1)
    logits = jnp.where(col_pos <= row_pos, logits, -jnp.inf)
    return jax.nn.softmax(logits, axis=-1).astype(BF16)


def shift(value, axis, by):
    length = lax.axis_size(axis)
    return lax.ppermute(value, axis, [(i, (i + by) % length) for i in range(length)])


def hand_down(value, section):
    length = lax.axis_size("section")
    half = length // 2
    if section % 2:
        pairs = [(i, i ^ 1) for i in range(length)]
    else:
        lows = [section - 1] if section == half else [
            i for i in range(1, length - 1, 2) if i != half - 1
        ]
        other = {i: i for i in range(length)}
        for low in lows:
            other[low], other[low + 1] = low + 1, low
        pairs = sorted(other.items())
    return lax.ppermute(value, "section", pairs)


def copies_kernel(value_ref, out_ref):
    for c in range(out_ref.shape[0]):
        out_ref[c] = value_ref[...]


def blocks_of_all(value):
    shape = (lax.axis_size("tensor"),) + value.shape
    copies = pl.pallas_call(
        copies_kernel,
        in_specs=[pl.BlockSpec(memory_space=pltpu.VMEM)],
        out_specs=pl.BlockSpec(memory_space=pltpu.VMEM),
        out_shape=jax.ShapeDtypeStruct(shape, value.dtype),
        compiler_params=pltpu.CompilerParams(vmem_limit_bytes=6 << 20),
        cost_estimate=pl.CostEstimate(
            flops=0, bytes_accessed=2 * math.prod(shape), transcendentals=0
        ),
        name="copies",
    )(value)
    return lax.all_to_all(copies, "tensor", 0, 0)


def transpose_kernel(value_ref, out_ref):
    out_ref[...] = value_ref[...].T


def transposed(value, tile=512, first=0, count=None):
    rows, columns = value.shape
    count = columns // tile if count is None else count
    return pl.pallas_call(
        transpose_kernel,
        grid=(count,),
        in_specs=[pl.BlockSpec((rows, tile), lambda i: (0, i + first))],
        out_specs=pl.BlockSpec((tile, rows), lambda i: (i, 0)),
        out_shape=jax.ShapeDtypeStruct((count * tile, rows), value.dtype),
        compiler_params=pltpu.CompilerParams(vmem_limit_bytes=12 << 20),
        cost_estimate=pl.CostEstimate(
            flops=0, bytes_accessed=4 * rows * count * tile, transcendentals=0
        ),
        name="transposed",
    )(value)


def place_kernel(spots, given, index_ref, *refs):
    pieces, out_ref, sems = refs[:given], refs[-2], refs[-1]
    copies = []
    for i, (piece, (slot, row)) in enumerate(zip(pieces, spots)):
        goal = out_ref.at[index_ref[slot], pl.ds(row, piece.shape[0])]
        copies.append(pltpu.make_async_copy(piece, goal, sems.at[i]))
    for copy in copies:
        copy.start()
    for copy in copies:
        copy.wait()


def put(index, pieces, shape, whole=None):
    arrays = [piece[0] for piece in pieces]
    spots = [piece[1:] for piece in pieces]
    more = [] if whole is None else [whole]
    return pl.pallas_call(
        functools.partial(place_kernel, spots, len(arrays)),
        in_specs=[pl.BlockSpec(memory_space=pltpu.SMEM)]
        + [pl.BlockSpec(memory_space=pl.ANY)] * (len(arrays) + len(more)),
        out_specs=pl.BlockSpec(memory_space=pl.ANY),
        out_shape=jax.ShapeDtypeStruct(shape, arrays[0].dtype),
        scratch_shapes=[pltpu.SemaphoreType.DMA((len(arrays),))],
        input_output_aliases={1 + len(arrays): 0} if more else {},
        compiler_params=pltpu.CompilerParams(vmem_limit_bytes=1 << 20),
        cost_estimate=pl.CostEstimate(
            flops=0,
            bytes_accessed=4 * sum(math.prod(array.shape) for array in arrays),
            transcendentals=0,
        ),
        name="put",
    )(index, *arrays, *more)


def across(value, x_by=0, z_by=0):
    length = lax.axis_size("tensor")
    xs = length // 2
    pairs = []
    for i in range(length):
        z, x = divmod(i, xs)
        pairs.append((i, (z + z_by) % 2 * xs + (x + x_by) % xs))
    return lax.ppermute(value, "tensor", pairs)


def gather_back(index, whole, halves, beside):
    n, k = whole.shape
    half = n // 2
    low, high = halves
    other = across(whole, 0, 1)
    left_low, right_low = across(low, 1), across(low, -1)
    left_high, right_high = across(high, 1), across(high, -1)
    first = (other, left_low, right_low, left_high, right_high)
    first, beside = lax.optimization_barrier((first, beside))
    other, left_low, right_low, left_high, right_high = first
    cross_left, cross_right = across(left_high, 0, 1), across(right_high, 0, 1)
    far_high, far_low = across(right_high, -1), across(left_low, 1)
    next_left, next_right = across(other[:half], 1), across(other[:half], -1)
    early = [
        (whole, 0, 0), (left_low, 1, 0), (left_high, 1, half),
        (right_low, 2, 0), (right_high, 2, half), (other, 4, 0),
    ]
    late = [
        (far_low, 3, 0), (far_high, 3, half),
        (next_left, 5, 0), (cross_left, 5, half), (next_right, 6, 0), (cross_right, 6, half),
        (across(next_left, 1), 7, 0), (across(far_high, 0, 1), 7, half),
    ]
    shape = (lax.axis_size("tensor"), n, k)
    whole, far_high = lax.optimization_barrier((whole, far_high))
    early[0], late[1] = (whole, 0, 0), (far_high, 3, half)
    return put(index, late, shape, put(index, early, shape)), beside


def value_grad_of(total, probs_t_ref, value_ref):
    attn = total.astype(BF16)
    micro_batch, length, depth = probs_t_ref.shape
    head_size = value_ref.shape[1]
    for m in range(micro_batch):
        rows = slice(m * length, (m + 1) * length)
        heads = [
            attn[rows, g * head_size : (g + 1) * head_size] for g in range(depth // length)
        ]
        value_ref[rows, :] = lax.dot_general(
            probs_t_ref[m], jnp.concatenate(heads, 0), NN, preferred_element_type=F32
        ).astype(BF16)


def keep(step, block, saved_ref, sem):
    copy = pltpu.make_async_copy(block, saved_ref.at[step], sem)
    copy.start()
    copy.wait()


def plain_kernel(
    steps, section, place_ref, rows_ref, weight_ref, probs_t_ref, kept_ref,
    value_ref, saved_ref, total, sem,
):
    step = pl.program_id(0)

    @pl.when(step == 0)
    def _():
        total[...] = jnp.zeros_like(total)

    total[...] += lax.dot_general(rows_ref[0], weight_ref[...], NN, preferred_element_type=F32)

    @pl.when(place_ref[0] == section)
    def _():
        keep(step, rows_ref.at[0], saved_ref, sem)

    @pl.when(step == steps - 1)
    def _():
        value_grad_of(total[...], probs_t_ref, value_ref)


def turn_kernel(
    first, steps, section, has_total, ends, place_ref, blocks_ref, *refs,
):
    refs = list(refs)
    count = len(steps)
    rows_refs = [refs.pop(0) for _ in range(count)]
    back_ref, weight_ref, probs_t_ref, kept_ref = (refs.pop(0) for _ in range(4))
    total_ref = refs.pop(0) if has_total else None
    new_refs = [refs.pop(0) for _ in range(count)]
    result_ref, saved_ref, heads, total, sem = refs
    step = pl.program_id(0)
    head_size = blocks_ref.shape[2]

    @pl.when(step == 0)
    def _():
        for c in range(blocks_ref.shape[0]):
            heads[:, c * head_size : (c + 1) * head_size] = blocks_ref[c]
        total[...] = total_ref[...] if has_total else jnp.zeros_like(total)

    branch = lax.dot_general(heads[...], back_ref[0], NN, preferred_element_type=F32)

    def finish(rows_ref, new_ref):
        new_rows = (rows_ref[0].astype(F32) + branch).astype(BF16)
        new_ref[0] = new_rows
        total[...] += lax.dot_general(
            new_rows, weight_ref[...], NN, preferred_element_type=F32
        )

        @pl.when(place_ref[0] == section)
        def _():
            keep(first + step, new_ref.at[0], saved_ref, sem)

    if count == 1:
        finish(rows_refs[0], new_refs[0])
    else:
        pl.when(step < steps[0])(lambda: finish(rows_refs[0], new_refs[0]))
        pl.when(step >= steps[0])(lambda: finish(rows_refs[1], new_refs[1]))

    @pl.when(step == sum(steps) - 1)
    def _():
        if ends:
            value_grad_of(total[...], probs_t_ref, result_ref)
        else:
            result_ref[...] = total[...]


def params():
    return pltpu.CompilerParams(vmem_limit_bytes=16 << 20)


def plain_turn(section, place, rows, weight_t, probs_t, saved):
    steps, count, tile = rows.shape
    own = weight_t.shape[1]
    head_size = 128
    return pl.pallas_call(
        functools.partial(plain_kernel, steps, section),
        grid=(steps,),
        in_specs=[
            pl.BlockSpec(memory_space=pltpu.SMEM),
            pl.BlockSpec((1, count, tile), lambda i: (i, 0, 0)),
            pl.BlockSpec((tile, own), lambda i: (i, 0)),
            pl.BlockSpec(probs_t.shape, lambda i: (0, 0, 0)),
            pl.BlockSpec(memory_space=pl.ANY),
        ],
        out_specs=[
            pl.BlockSpec((count, head_size), lambda i: (0, 0)),
            pl.BlockSpec(memory_space=pl.ANY),
        ],
        out_shape=[
            jax.ShapeDtypeStruct((count, head_size), BF16),
            jax.ShapeDtypeStruct(saved.shape, BF16),
        ],
        scratch_shapes=[pltpu.VMEM((count, own), F32), pltpu.SemaphoreType.DMA],
        input_output_aliases={4: 1},
        compiler_params=params(),
        cost_estimate=pl.CostEstimate(
            flops=2 * steps * count * tile * own,
            bytes_accessed=2 * steps * tile * own,
            transcendentals=0,
        ),
        name="plain_turn",
    )(place, rows, weight_t, probs_t, saved)


def turn(section, place, blocks, rows, back, weight_t, probs_t, saved, first=0, total=None, ends=True):
    count, tile = rows[0].shape[1:]
    own = weight_t.shape[1]
    depth = back.shape[1]
    head_size = blocks.shape[2]
    steps = [part.shape[0] for part in rows]
    parts = [pl.BlockSpec((1, count, tile), lambda i: (jnp.minimum(i, steps[0] - 1), 0, 0))]
    if len(rows) == 2:
        parts.append(
            pl.BlockSpec((1, count, tile), lambda i: (jnp.maximum(i - steps[0], 0), 0, 0))
        )
    whole = pl.BlockSpec((count, own), lambda i: (0, 0))
    extra = [] if total is None else [total]
    if ends:
        result = jax.ShapeDtypeStruct((count, head_size), BF16)
    else:
        result = jax.ShapeDtypeStruct((count, own), F32)
    alias = 5 + len(rows)
    outs = pl.pallas_call(
        functools.partial(turn_kernel, first, steps, section, total is not None, ends),
        grid=(sum(steps),),
        in_specs=[
            pl.BlockSpec(memory_space=pltpu.SMEM),
            pl.BlockSpec(blocks.shape, lambda i: (0, 0, 0)),
            *parts,
            pl.BlockSpec((1, depth, tile), lambda i: (i + first, 0, 0)),
            pl.BlockSpec((tile, own), lambda i: (i + first, 0)),
            pl.BlockSpec(probs_t.shape, lambda i: (0, 0, 0)),
            pl.BlockSpec(memory_space=pl.ANY),
            *[whole for _ in extra],
        ],
        out_specs=[
            *parts,
            pl.BlockSpec(result.shape, lambda i: (0, 0)),
            pl.BlockSpec(memory_space=pl.ANY),
        ],
        out_shape=[
            *[jax.ShapeDtypeStruct(part.shape, BF16) for part in rows],
            result,
            jax.ShapeDtypeStruct(saved.shape, BF16),
        ],
        scratch_shapes=[
            pltpu.VMEM((count, depth), BF16),
            pltpu.VMEM((count, own), F32),
            pltpu.SemaphoreType.DMA,
        ],
        input_output_aliases={alias: len(rows) + 1},
        compiler_params=params(),
        cost_estimate=pl.CostEstimate(
            flops=2 * sum(steps) * count * tile * (own + depth),
            bytes_accessed=2 * sum(steps) * tile * (own + depth),
            transcendentals=0,
        ),
        name="turn",
    )(place, blocks, *rows, back, weight_t, probs_t, saved, *extra)
    return outs[:-2], outs[-2], outs[-1]


def pick_kernel(me_ref, rows_ref, out_ref):
    out_ref[...] = rows_ref[0]


def pick(me, rows):
    _, count, tile = rows.shape
    return pl.pallas_call(
        pick_kernel,
        grid_spec=pltpu.PrefetchScalarGridSpec(
            num_scalar_prefetch=1,
            grid=(1,),
            in_specs=[pl.BlockSpec((1, count, tile), lambda i, me: (me[0], 0, 0))],
            out_specs=pl.BlockSpec((count, tile), lambda i, me: (0, 0)),
        ),
        out_shape=jax.ShapeDtypeStruct((count, tile), rows.dtype),
        compiler_params=pltpu.CompilerParams(vmem_limit_bytes=4 << 20),
        name="pick",
    )(me, rows)


def last_kernel(place_ref, me_ref, blocks_ref, rows_ref, value_t_ref, above_ref, out_ref, heads):
    head_size = blocks_ref.shape[2]

    @pl.when(place_ref[0] == 0)
    def _():
        for c in range(blocks_ref.shape[0]):
            heads[:, c * head_size : (c + 1) * head_size] = blocks_ref[c]
        branch = lax.dot_general(heads[...], value_t_ref[...], NN, preferred_element_type=F32)
        out_ref[...] = (rows_ref[0].astype(F32) + branch).astype(BF16)

    @pl.when(place_ref[0] != 0)
    def _():
        out_ref[...] = above_ref[...]


def last_features(place, me, blocks, rows, value_t, above):
    _, count, tile = rows.shape
    depth = value_t.shape[0]
    return pl.pallas_call(
        last_kernel,
        grid_spec=pltpu.PrefetchScalarGridSpec(
            num_scalar_prefetch=2,
            grid=(1,),
            in_specs=[
                pl.BlockSpec(blocks.shape, lambda i, place, me: (0, 0, 0)),
                pl.BlockSpec((1, count, tile), lambda i, place, me: (me[0], 0, 0)),
                pl.BlockSpec(value_t.shape, lambda i, place, me: (0, 0)),
                pl.BlockSpec((count, tile), lambda i, place, me: (0, 0)),
            ],
            out_specs=pl.BlockSpec((count, tile), lambda i, place, me: (0, 0)),
            scratch_shapes=[pltpu.VMEM((count, depth), BF16)],
        ),
        out_shape=jax.ShapeDtypeStruct((count, tile), BF16),
        compiler_params=params(),
        cost_estimate=pl.CostEstimate(
            flops=2 * count * tile * depth, bytes_accessed=2 * tile * depth, transcendentals=0
        ),
        name="last_features",
    )(place, me, blocks, rows, value_t, above)


def weight_kernel(mixed_t_ref, rows_ref, out_ref):
    out_ref[...] = lax.dot_general(
        mixed_t_ref[...], rows_ref[0], NN, preferred_element_type=F32
    ).astype(BF16)


def weight_grads(mixed_t, rows):
    steps, count, tile = rows.shape
    own = mixed_t.shape[0]
    return pl.pallas_call(
        weight_kernel,
        grid=(steps,),
        in_specs=[
            pl.BlockSpec((own, count), lambda i: (0, 0)),
            pl.BlockSpec((1, count, tile), lambda i: (i, 0, 0)),
        ],
        out_specs=pl.BlockSpec((own, tile), lambda i: (0, i)),
        out_shape=jax.ShapeDtypeStruct((own, steps * tile), BF16),
        compiler_params=params(),
        cost_estimate=pl.CostEstimate(
            flops=2 * steps * count * tile * own,
            bytes_accessed=2 * steps * tile * own,
            transcendentals=0,
        ),
        name="weight_grads",
    )(mixed_t, rows)


def on_device(grad_top, query, keys, values, out_weight, value_weight):
    sections = lax.axis_size("section")
    place = lax.axis_index("section")
    me = lax.axis_index("tensor")
    micro_batch, length = query.shape[1], query.shape[2]
    rows = micro_batch * length
    head_size = keys.shape[3]
    group = query.shape[3] // head_size
    feat_local = grad_top.shape[2]
    spot = place.astype(jnp.int32).reshape(1)
    mine = me.astype(jnp.int32).reshape(1)
    xs = lax.axis_size("tensor") // 2
    z, x = me // xs, me % xs
    index = jnp.stack(
        [
            (z + dz) % 2 * xs + (x + dx) % xs
            for dz in (0, 1)
            for dx in (0, -1, 1, 2)
        ]
    ).astype(jnp.int32)
    value_t = transposed(value_weight[0])
    top, value_t = lax.optimization_barrier((grad_top.reshape(rows, feat_local), value_t))
    whole = lax.ppermute(value_t, "section", [(i, i - 1) for i in range(1, sections)])
    incoming = blocks_of_all(top)
    query_heads = query[0].reshape(micro_batch, length, group, head_size)
    probs = jax.vmap(causal_probs)(query_heads, keys[0])
    mixed = jnp.einsum("mgqp,mpd->mqgd", probs, values[0], preferred_element_type=F32)
    mixed_t = transposed(mixed.astype(BF16).reshape(rows, group * head_size), group * head_size)
    probs_t = probs.transpose(0, 3, 1, 2).reshape(micro_batch, length, group * length)
    weight_t = transposed(out_weight[0])
    half = whole.shape[0] // 2
    whole, incoming, index, spot, mine = lax.optimization_barrier(
        (whole, incoming, index, spot, mine)
    )
    halves = lax.optimization_barrier((whole[:half], whole[half:]))
    value_grad, saved = plain_turn(
        sections - 1, spot, incoming, weight_t, probs_t, jnp.zeros_like(incoming)
    )
    beside = (incoming, value_grad, saved, mixed_t, probs_t, weight_t, value_t)
    back, beside = gather_back(index, whole, halves, beside)
    incoming, value_grad, saved, mixed_t, probs_t, weight_t, value_t = beside
    back, value_grad = lax.optimization_barrier((back, value_grad))
    parts = (incoming[:AHEAD], incoming[AHEAD:])
    for section in range(sections - 1, 0, -1):
        moved = hand_down(value_grad, section)
        parts, moved = lax.optimization_barrier((parts, moved))
        parts = [hand_down(part, section) for part in parts]
        blocks = blocks_of_all(moved)
        below = section - 1
        if section % 2:
            parts, value_grad, saved = turn(
                below, spot, blocks, parts, back, weight_t, probs_t, saved
            )
        else:
            (ahead,), total, saved = turn(
                below, spot, blocks, parts[:1], back, weight_t, probs_t, saved, ends=False
            )
            (rest,), value_grad, saved = turn(
                below, spot, blocks, parts[1:], back, weight_t, probs_t, saved, AHEAD, total
            )
            parts = (ahead, rest)
    above = shift(pick(mine, saved), "section", 1)
    grads = last_features(spot, mine, blocks_of_all(value_grad), saved, value_t, above)
    return (
        grads.reshape(1, micro_batch, length, feat_local),
        weight_grads(mixed_t, saved)[None],
    )


def solution(mesh):
    placed = (
        P(None, None, "tensor"),
        P("section", None, None, "tensor"),
        P("section", None, None, "tensor"),
        P("section", None, None, "tensor"),
        P("section", "tensor", None),
        P("section", "tensor", None),
    )
    return jax.shard_map(
        on_device,
        mesh=mesh,
        in_specs=placed,
        out_specs=(P("section", None, None, "tensor"), P("section", "tensor", None)),
        check_vma=False,
    )
```

```python
import functools
import math

import jax
import jax.numpy as jnp
from jax import lax
from jax.experimental import pallas as pl
from jax.experimental.pallas import tpu as pltpu
from jax.sharding import PartitionSpec as P

F32 = jnp.float32
BF16 = jnp.bfloat16
NN = (((1,), (0,)), ((), ()))


AHEAD = 5


def causal_probs(query_heads, key_rows):
    head_size = key_rows.shape[-1]
    length = key_rows.shape[0]
    logits = jnp.einsum("qgd,pd->gqp", query_heads, key_rows, preferred_element_type=F32)
    logits = logits * (1.0 / math.sqrt(head_size))
    row_pos = lax.broadcasted_iota(jnp.int32, (length, length), 0)
    col_pos = lax.broadcasted_iota(jnp.int32, (length, length), 1)
    logits = jnp.where(col_pos <= row_pos, logits, -jnp.inf)
    return jax.nn.softmax(logits, axis=-1).astype(BF16)


def shift(value, axis, by):
    length = lax.axis_size(axis)
    return lax.ppermute(value, axis, [(i, (i + by) % length) for i in range(length)])


def hand_down(value, section):
    length = lax.axis_size("section")
    half = length // 2
    if section % 2:
        pairs = [(i, i ^ 1) for i in range(length)]
    else:
        lows = [section - 1] if section == half else [
            i for i in range(1, length - 1, 2) if i != half - 1
        ]
        other = {i: i for i in range(length)}
        for low in lows:
            other[low], other[low + 1] = low + 1, low
        pairs = sorted(other.items())
    return lax.ppermute(value, "section", pairs)


def copies_kernel(value_ref, out_ref):
    for c in range(out_ref.shape[0]):
        out_ref[c] = value_ref[...]


def blocks_of_all(value):
    shape = (lax.axis_size("tensor"),) + value.shape
    copies = pl.pallas_call(
        copies_kernel,
        in_specs=[pl.BlockSpec(memory_space=pltpu.VMEM)],
        out_specs=pl.BlockSpec(memory_space=pltpu.VMEM),
        out_shape=jax.ShapeDtypeStruct(shape, value.dtype),
        compiler_params=pltpu.CompilerParams(vmem_limit_bytes=6 << 20),
        cost_estimate=pl.CostEstimate(
            flops=0, bytes_accessed=2 * math.prod(shape), transcendentals=0
        ),
        name="copies",
    )(value)
    return lax.all_to_all(copies, "tensor", 0, 0)


def transpose_kernel(value_ref, out_ref):
    out_ref[...] = value_ref[...].T


def transposed(value, tile=512, first=0, count=None):
    rows, columns = value.shape
    count = columns // tile if count is None else count
    return pl.pallas_call(
        transpose_kernel,
        grid=(count,),
        in_specs=[pl.BlockSpec((rows, tile), lambda i: (0, i + first))],
        out_specs=pl.BlockSpec((tile, rows), lambda i: (i, 0)),
        out_shape=jax.ShapeDtypeStruct((count * tile, rows), value.dtype),
        compiler_params=pltpu.CompilerParams(vmem_limit_bytes=12 << 20),
        cost_estimate=pl.CostEstimate(
            flops=0, bytes_accessed=4 * rows * count * tile, transcendentals=0
        ),
        name="transposed",
    )(value)


def place_kernel(spots, given, index_ref, *refs):
    pieces, out_ref, sems = refs[:given], refs[-2], refs[-1]
    copies = []
    for piece, (slot, runs) in zip(pieces, spots):
        for source, length, goal in runs:
            copies.append(
                pltpu.make_async_copy(
                    piece.at[pl.ds(source, length)],
                    out_ref.at[index_ref[slot], pl.ds(goal, length)],
                    sems.at[len(copies)],
                )
            )
    for copy in copies:
        copy.start()
    for copy in copies:
        copy.wait()


def put(index, pieces, shape, whole=None):
    arrays = [piece[0] for piece in pieces]
    spots = [piece[1:] for piece in pieces]
    more = [] if whole is None else [whole]
    return pl.pallas_call(
        functools.partial(place_kernel, spots, len(arrays)),
        in_specs=[pl.BlockSpec(memory_space=pltpu.SMEM)]
        + [pl.BlockSpec(memory_space=pl.ANY)] * (len(arrays) + len(more)),
        out_specs=pl.BlockSpec(memory_space=pl.ANY),
        out_shape=jax.ShapeDtypeStruct(shape, arrays[0].dtype),
        scratch_shapes=[pltpu.SemaphoreType.DMA((sum(len(runs) for _, runs in spots),))],
        input_output_aliases={1 + len(arrays): 0} if more else {},
        compiler_params=pltpu.CompilerParams(vmem_limit_bytes=1 << 20),
        cost_estimate=pl.CostEstimate(
            flops=0,
            bytes_accessed=4 * sum(math.prod(array.shape) for array in arrays),
            transcendentals=0,
        ),
        name="put",
    )(index, *arrays, *more)


def across(value, x_by=0, z_by=0):
    length = lax.axis_size("tensor")
    xs = length // 2
    pairs = []
    for i in range(length):
        z, x = divmod(i, xs)
        pairs.append((i, (z + z_by) % 2 * xs + (x + x_by) % xs))
    return lax.ppermute(value, "tensor", pairs)


def gather_both(index, back, top, beside):
    n, k = back.shape
    m = top.shape[0]
    whole = jnp.concatenate([back[: n // 2], top[: m // 2], back[n // 2 :], top[m // 2 :]])
    whole = lax.optimization_barrier(whole)
    half = (n + m) // 2
    low, high = lax.optimization_barrier((whole[:half], whole[half:]))
    other = across(whole, 0, 1)
    left_low, right_low = across(low, 1), across(low, -1)
    left_high, right_high = across(high, 1), across(high, -1)
    first = (other, left_low, right_low, left_high, right_high)
    first, beside = lax.optimization_barrier((first, beside))
    other, left_low, right_low, left_high, right_high = first
    cross_left, cross_right = across(left_high, 0, 1), across(right_high, 0, 1)
    far_high, far_low = across(right_high, -1), across(left_low, 1)
    next_left, next_right = across(other[:half], 1), across(other[:half], -1)
    whole, far_high = lax.optimization_barrier((whole, far_high))
    lows = [(0, n // 2, 0), (n // 2, m // 2, n)]
    highs = [(0, n // 2, n // 2), (n // 2, m // 2, n + m // 2)]
    both = lows + [(half + source, length, goal) for source, length, goal in highs]
    early = [
        (whole, 0, both), (left_low, 1, lows), (left_high, 1, highs),
        (right_low, 2, lows), (right_high, 2, highs), (other, 4, both),
    ]
    late = [
        (far_low, 3, lows), (far_high, 3, highs),
        (next_left, 5, lows), (cross_left, 5, highs),
        (next_right, 6, lows), (cross_right, 6, highs),
        (across(next_left, 1), 7, lows), (across(far_high, 0, 1), 7, highs),
    ]
    shape = (lax.axis_size("tensor"), n + m, k)
    return put(index, late, shape, put(index, early, shape)), beside


def value_grad_of(total, probs_t_ref, value_ref):
    attn = total.astype(BF16)
    micro_batch, length, depth = probs_t_ref.shape
    head_size = value_ref.shape[1]
    for m in range(micro_batch):
        rows = slice(m * length, (m + 1) * length)
        heads = [
            attn[rows, g * head_size : (g + 1) * head_size] for g in range(depth // length)
        ]
        value_ref[rows, :] = lax.dot_general(
            probs_t_ref[m], jnp.concatenate(heads, 0), NN, preferred_element_type=F32
        ).astype(BF16)


def keep(step, block, saved_ref, sem):
    copy = pltpu.make_async_copy(block, saved_ref.at[step], sem)
    copy.start()
    copy.wait()


def plain_kernel(
    steps, section, place_ref, rows_ref, weight_ref, probs_t_ref, kept_ref,
    value_ref, saved_ref, total, sem,
):
    step = pl.program_id(0)

    @pl.when(step == 0)
    def _():
        total[...] = jnp.zeros_like(total)

    total[...] += lax.dot_general(rows_ref[0], weight_ref[...], NN, preferred_element_type=F32)

    @pl.when(place_ref[0] == section)
    def _():
        keep(step, rows_ref.at[0], saved_ref, sem)

    @pl.when(step == steps - 1)
    def _():
        value_grad_of(total[...], probs_t_ref, value_ref)


def turn_kernel(
    first, steps, section, has_total, ends, place_ref, blocks_ref, *refs,
):
    refs = list(refs)
    count = len(steps)
    rows_refs = [refs.pop(0) for _ in range(count)]
    back_ref, weight_ref, probs_t_ref, kept_ref = (refs.pop(0) for _ in range(4))
    total_ref = refs.pop(0) if has_total else None
    new_refs = [refs.pop(0) for _ in range(count)]
    result_ref, saved_ref, heads, total, sem = refs
    step = pl.program_id(0)
    head_size = blocks_ref.shape[2]

    @pl.when(step == 0)
    def _():
        for c in range(blocks_ref.shape[0]):
            heads[:, c * head_size : (c + 1) * head_size] = blocks_ref[c]
        total[...] = total_ref[...] if has_total else jnp.zeros_like(total)

    branch = lax.dot_general(heads[...], back_ref[0], NN, preferred_element_type=F32)

    def finish(rows_ref, new_ref):
        new_rows = (rows_ref[0].astype(F32) + branch).astype(BF16)
        new_ref[0] = new_rows
        total[...] += lax.dot_general(
            new_rows, weight_ref[...], NN, preferred_element_type=F32
        )

        @pl.when(place_ref[0] == section)
        def _():
            keep(first + step, new_ref.at[0], saved_ref, sem)

    if count == 1:
        finish(rows_refs[0], new_refs[0])
    else:
        pl.when(step < steps[0])(lambda: finish(rows_refs[0], new_refs[0]))
        pl.when(step >= steps[0])(lambda: finish(rows_refs[1], new_refs[1]))

    @pl.when(step == sum(steps) - 1)
    def _():
        if ends:
            value_grad_of(total[...], probs_t_ref, result_ref)
        else:
            result_ref[...] = total[...]


def params():
    return pltpu.CompilerParams(vmem_limit_bytes=16 << 20)


def plain_turn(section, place, both, count, weight_t, probs_t, saved):
    steps, length, tile = both.shape
    own = weight_t.shape[1]
    head_size = 128
    return pl.pallas_call(
        functools.partial(plain_kernel, steps, section),
        grid=(steps,),
        in_specs=[
            pl.BlockSpec(memory_space=pltpu.SMEM),
            pl.BlockSpec((1, count, tile), lambda i: (i, length // count - 1, 0)),
            pl.BlockSpec((tile, own), lambda i: (i, 0)),
            pl.BlockSpec(probs_t.shape, lambda i: (0, 0, 0)),
            pl.BlockSpec(memory_space=pl.ANY),
        ],
        out_specs=[
            pl.BlockSpec((count, head_size), lambda i: (0, 0)),
            pl.BlockSpec(memory_space=pl.ANY),
        ],
        out_shape=[
            jax.ShapeDtypeStruct((count, head_size), BF16),
            jax.ShapeDtypeStruct(saved.shape, BF16),
        ],
        scratch_shapes=[pltpu.VMEM((count, own), F32), pltpu.SemaphoreType.DMA],
        input_output_aliases={4: 1},
        compiler_params=params(),
        cost_estimate=pl.CostEstimate(
            flops=2 * steps * count * tile * own,
            bytes_accessed=2 * steps * tile * own,
            transcendentals=0,
        ),
        name="plain_turn",
    )(place, both, weight_t, probs_t, saved)


def turn(section, place, blocks, rows, back, weight_t, probs_t, saved, first=0, total=None, ends=True):
    count, tile = rows[0].shape[1:]
    own = weight_t.shape[1]
    head_size = blocks.shape[2]
    depth = blocks.shape[0] * head_size
    steps = [part.shape[0] for part in rows]
    parts = [pl.BlockSpec((1, count, tile), lambda i: (jnp.minimum(i, steps[0] - 1), 0, 0))]
    if len(rows) == 2:
        parts.append(
            pl.BlockSpec((1, count, tile), lambda i: (jnp.maximum(i - steps[0], 0), 0, 0))
        )
    whole = pl.BlockSpec((count, own), lambda i: (0, 0))
    extra = [] if total is None else [total]
    if ends:
        result = jax.ShapeDtypeStruct((count, head_size), BF16)
    else:
        result = jax.ShapeDtypeStruct((count, own), F32)
    alias = 5 + len(rows)
    outs = pl.pallas_call(
        functools.partial(turn_kernel, first, steps, section, total is not None, ends),
        grid=(sum(steps),),
        in_specs=[
            pl.BlockSpec(memory_space=pltpu.SMEM),
            pl.BlockSpec(blocks.shape, lambda i: (0, 0, 0)),
            *parts,
            pl.BlockSpec((1, depth, tile), lambda i: (i + first, 0, 0)),
            pl.BlockSpec((tile, own), lambda i: (i + first, 0)),
            pl.BlockSpec(probs_t.shape, lambda i: (0, 0, 0)),
            pl.BlockSpec(memory_space=pl.ANY),
            *[whole for _ in extra],
        ],
        out_specs=[
            *parts,
            pl.BlockSpec(result.shape, lambda i: (0, 0)),
            pl.BlockSpec(memory_space=pl.ANY),
        ],
        out_shape=[
            *[jax.ShapeDtypeStruct(part.shape, BF16) for part in rows],
            result,
            jax.ShapeDtypeStruct(saved.shape, BF16),
        ],
        scratch_shapes=[
            pltpu.VMEM((count, depth), BF16),
            pltpu.VMEM((count, own), F32),
            pltpu.SemaphoreType.DMA,
        ],
        input_output_aliases={alias: len(rows) + 1},
        compiler_params=params(),
        cost_estimate=pl.CostEstimate(
            flops=2 * sum(steps) * count * tile * (own + depth),
            bytes_accessed=2 * sum(steps) * tile * (own + depth),
            transcendentals=0,
        ),
        name="turn",
    )(place, blocks, *rows, back, weight_t, probs_t, saved, *extra)
    return outs[:-2], outs[-2], outs[-1]


def pick_kernel(me_ref, rows_ref, out_ref):
    out_ref[...] = rows_ref[0]


def pick(me, rows):
    _, count, tile = rows.shape
    return pl.pallas_call(
        pick_kernel,
        grid_spec=pltpu.PrefetchScalarGridSpec(
            num_scalar_prefetch=1,
            grid=(1,),
            in_specs=[pl.BlockSpec((1, count, tile), lambda i, me: (me[0], 0, 0))],
            out_specs=pl.BlockSpec((count, tile), lambda i, me: (0, 0)),
        ),
        out_shape=jax.ShapeDtypeStruct((count, tile), rows.dtype),
        compiler_params=pltpu.CompilerParams(vmem_limit_bytes=4 << 20),
        name="pick",
    )(me, rows)


def last_kernel(place_ref, me_ref, blocks_ref, rows_ref, value_t_ref, above_ref, out_ref, heads):
    head_size = blocks_ref.shape[2]

    @pl.when(place_ref[0] == 0)
    def _():
        for c in range(blocks_ref.shape[0]):
            heads[:, c * head_size : (c + 1) * head_size] = blocks_ref[c]
        branch = lax.dot_general(heads[...], value_t_ref[...], NN, preferred_element_type=F32)
        out_ref[...] = (rows_ref[0].astype(F32) + branch).astype(BF16)

    @pl.when(place_ref[0] != 0)
    def _():
        out_ref[...] = above_ref[...]


def last_features(place, me, blocks, rows, value_t, above):
    _, count, tile = rows.shape
    depth = value_t.shape[0]
    return pl.pallas_call(
        last_kernel,
        grid_spec=pltpu.PrefetchScalarGridSpec(
            num_scalar_prefetch=2,
            grid=(1,),
            in_specs=[
                pl.BlockSpec(blocks.shape, lambda i, place, me: (0, 0, 0)),
                pl.BlockSpec((1, count, tile), lambda i, place, me: (me[0], 0, 0)),
                pl.BlockSpec(value_t.shape, lambda i, place, me: (0, 0)),
                pl.BlockSpec((count, tile), lambda i, place, me: (0, 0)),
            ],
            out_specs=pl.BlockSpec((count, tile), lambda i, place, me: (0, 0)),
            scratch_shapes=[pltpu.VMEM((count, depth), BF16)],
        ),
        out_shape=jax.ShapeDtypeStruct((count, tile), BF16),
        compiler_params=params(),
        cost_estimate=pl.CostEstimate(
            flops=2 * count * tile * depth, bytes_accessed=2 * tile * depth, transcendentals=0
        ),
        name="last_features",
    )(place, me, blocks, rows, value_t, above)


def weight_kernel(mixed_t_ref, rows_ref, out_ref):
    out_ref[...] = lax.dot_general(
        mixed_t_ref[...], rows_ref[0], NN, preferred_element_type=F32
    ).astype(BF16)


def weight_grads(mixed_t, rows):
    steps, count, tile = rows.shape
    own = mixed_t.shape[0]
    return pl.pallas_call(
        weight_kernel,
        grid=(steps,),
        in_specs=[
            pl.BlockSpec((own, count), lambda i: (0, 0)),
            pl.BlockSpec((1, count, tile), lambda i: (i, 0, 0)),
        ],
        out_specs=pl.BlockSpec((own, tile), lambda i: (0, i)),
        out_shape=jax.ShapeDtypeStruct((own, steps * tile), BF16),
        compiler_params=params(),
        cost_estimate=pl.CostEstimate(
            flops=2 * steps * count * tile * own,
            bytes_accessed=2 * steps * tile * own,
            transcendentals=0,
        ),
        name="weight_grads",
    )(mixed_t, rows)


def on_device(grad_top, query, keys, values, out_weight, value_weight):
    sections = lax.axis_size("section")
    place = lax.axis_index("section")
    me = lax.axis_index("tensor")
    micro_batch, length = query.shape[1], query.shape[2]
    rows = micro_batch * length
    head_size = keys.shape[3]
    group = query.shape[3] // head_size
    feat_local = grad_top.shape[2]
    spot = place.astype(jnp.int32).reshape(1)
    mine = me.astype(jnp.int32).reshape(1)
    xs = lax.axis_size("tensor") // 2
    z, x = me // xs, me % xs
    index = jnp.stack(
        [
            (z + dz) % 2 * xs + (x + dx) % xs
            for dz in (0, 1)
            for dx in (0, -1, 1, 2)
        ]
    ).astype(jnp.int32)
    value_t = transposed(value_weight[0])
    back = lax.ppermute(value_t, "section", [(i, i - 1) for i in range(1, sections)])
    back, index, spot, mine = lax.optimization_barrier((back, index, spot, mine))
    query_heads = query[0].reshape(micro_batch, length, group, head_size)
    probs = jax.vmap(causal_probs)(query_heads, keys[0])
    mixed = jnp.einsum("mgqp,mpd->mqgd", probs, values[0], preferred_element_type=F32)
    mixed_t = transposed(mixed.astype(BF16).reshape(rows, group * head_size), group * head_size)
    probs_t = probs.transpose(0, 3, 1, 2).reshape(micro_batch, length, group * length)
    weight_t = transposed(out_weight[0])
    empty = jnp.zeros((lax.axis_size("tensor"), rows, feat_local), BF16)
    beside = (mixed_t, probs_t, weight_t, value_t, empty)
    both, beside = gather_both(index, back, grad_top.reshape(rows, feat_local), beside)
    mixed_t, probs_t, weight_t, value_t, empty = beside
    value_grad, saved = plain_turn(sections - 1, spot, both, rows, weight_t, probs_t, empty)
    parts = (both[:AHEAD, -rows:], both[AHEAD:, -rows:])
    for section in range(sections - 1, 0, -1):
        moved = hand_down(value_grad, section)
        parts, moved = lax.optimization_barrier((parts, moved))
        parts = [hand_down(part, section) for part in parts]
        blocks = blocks_of_all(moved)
        below = section - 1
        if section % 2:
            parts, value_grad, saved = turn(
                below, spot, blocks, parts, both, weight_t, probs_t, saved
            )
        else:
            (ahead,), total, saved = turn(
                below, spot, blocks, parts[:1], both, weight_t, probs_t, saved, ends=False
            )
            (rest,), value_grad, saved = turn(
                below, spot, blocks, parts[1:], both, weight_t, probs_t, saved, AHEAD, total
            )
            parts = (ahead, rest)
    above = shift(pick(mine, saved), "section", 1)
    grads = last_features(spot, mine, blocks_of_all(value_grad), saved, value_t, above)
    return (
        grads.reshape(1, micro_batch, length, feat_local),
        weight_grads(mixed_t, saved)[None],
    )


def solution(mesh):
    placed = (
        P(None, None, "tensor"),
        P("section", None, None, "tensor"),
        P("section", None, None, "tensor"),
        P("section", None, None, "tensor"),
        P("section", "tensor", None),
        P("section", "tensor", None),
    )
    return jax.shard_map(
        on_device,
        mesh=mesh,
        in_specs=placed,
        out_specs=(P("section", None, None, "tensor"), P("section", "tensor", None)),
        check_vma=False,
    )
```

```python
import functools
import math

import jax
import jax.numpy as jnp
from jax import lax
from jax.experimental import pallas as pl
from jax.experimental.pallas import tpu as pltpu
from jax.sharding import PartitionSpec as P

F32 = jnp.float32
BF16 = jnp.bfloat16
NN = (((1,), (0,)), ((), ()))


AHEAD = 5


def causal_probs(query_heads, key_rows):
    head_size = key_rows.shape[-1]
    length = key_rows.shape[0]
    logits = jnp.einsum("qgd,pd->gqp", query_heads, key_rows, preferred_element_type=F32)
    logits = logits * (1.0 / math.sqrt(head_size))
    row_pos = lax.broadcasted_iota(jnp.int32, (length, length), 0)
    col_pos = lax.broadcasted_iota(jnp.int32, (length, length), 1)
    logits = jnp.where(col_pos <= row_pos, logits, -jnp.inf)
    return jax.nn.softmax(logits, axis=-1).astype(BF16)


def shift(value, axis, by):
    length = lax.axis_size(axis)
    return lax.ppermute(value, axis, [(i, (i + by) % length) for i in range(length)])


def hand_down(value, section):
    length = lax.axis_size("section")
    half = length // 2
    if section % 2:
        pairs = [(i, i ^ 1) for i in range(length)]
    else:
        lows = [section - 1] if section == half else [
            i for i in range(1, length - 1, 2) if i != half - 1
        ]
        other = {i: i for i in range(length)}
        for low in lows:
            other[low], other[low + 1] = low + 1, low
        pairs = sorted(other.items())
    return lax.ppermute(value, "section", pairs)


def copies_kernel(value_ref, out_ref):
    for c in range(out_ref.shape[0]):
        out_ref[c] = value_ref[...]


def blocks_of_all(value):
    shape = (lax.axis_size("tensor"),) + value.shape
    copies = pl.pallas_call(
        copies_kernel,
        in_specs=[pl.BlockSpec(memory_space=pltpu.VMEM)],
        out_specs=pl.BlockSpec(memory_space=pltpu.VMEM),
        out_shape=jax.ShapeDtypeStruct(shape, value.dtype),
        compiler_params=pltpu.CompilerParams(vmem_limit_bytes=6 << 20),
        cost_estimate=pl.CostEstimate(
            flops=0, bytes_accessed=2 * math.prod(shape), transcendentals=0
        ),
        name="copies",
    )(value)
    return lax.all_to_all(copies, "tensor", 0, 0)


def transpose_kernel(value_ref, out_ref):
    out_ref[...] = value_ref[...].T


def transposed(value, tile=512, first=0, count=None):
    rows, columns = value.shape
    count = columns // tile if count is None else count
    return pl.pallas_call(
        transpose_kernel,
        grid=(count,),
        in_specs=[pl.BlockSpec((rows, tile), lambda i: (0, i + first))],
        out_specs=pl.BlockSpec((tile, rows), lambda i: (i, 0)),
        out_shape=jax.ShapeDtypeStruct((count * tile, rows), value.dtype),
        compiler_params=pltpu.CompilerParams(vmem_limit_bytes=12 << 20),
        cost_estimate=pl.CostEstimate(
            flops=0, bytes_accessed=4 * rows * count * tile, transcendentals=0
        ),
        name="transposed",
    )(value)


def place_kernel(spots, given, index_ref, *refs):
    pieces, out_ref, sems = refs[:given], refs[-2], refs[-1]
    copies = []
    for piece, (slot, runs) in zip(pieces, spots):
        for source, length, goal in runs:
            copies.append(
                pltpu.make_async_copy(
                    piece.at[pl.ds(source, length)],
                    out_ref.at[index_ref[slot], pl.ds(goal, length)],
                    sems.at[len(copies)],
                )
            )
    for copy in copies:
        copy.start()
    for copy in copies:
        copy.wait()


def put(index, pieces, shape, whole=None):
    arrays = [piece[0] for piece in pieces]
    spots = [piece[1:] for piece in pieces]
    more = [] if whole is None else [whole]
    return pl.pallas_call(
        functools.partial(place_kernel, spots, len(arrays)),
        in_specs=[pl.BlockSpec(memory_space=pltpu.SMEM)]
        + [pl.BlockSpec(memory_space=pl.ANY)] * (len(arrays) + len(more)),
        out_specs=pl.BlockSpec(memory_space=pl.ANY),
        out_shape=jax.ShapeDtypeStruct(shape, arrays[0].dtype),
        scratch_shapes=[pltpu.SemaphoreType.DMA((sum(len(runs) for _, runs in spots),))],
        input_output_aliases={1 + len(arrays): 0} if more else {},
        compiler_params=pltpu.CompilerParams(vmem_limit_bytes=1 << 20),
        cost_estimate=pl.CostEstimate(
            flops=0,
            bytes_accessed=4 * sum(math.prod(array.shape) for array in arrays),
            transcendentals=0,
        ),
        name="put",
    )(index, *arrays, *more)


def across(value, x_by=0, z_by=0):
    length = lax.axis_size("tensor")
    xs = length // 2
    pairs = []
    for i in range(length):
        z, x = divmod(i, xs)
        pairs.append((i, (z + z_by) % 2 * xs + (x + x_by) % xs))
    return lax.ppermute(value, "tensor", pairs)


def gather_both(index, back, top, beside):
    n, k = back.shape
    m = top.shape[0]
    whole = jnp.concatenate([back[: n // 2], top[: m // 2], back[n // 2 :], top[m // 2 :]])
    whole = lax.optimization_barrier(whole)
    half = (n + m) // 2
    low, high = lax.optimization_barrier((whole[:half], whole[half:]))
    other = across(whole, 0, 1)
    left_low, right_low = across(low, 1), across(low, -1)
    left_high, right_high = across(high, 1), across(high, -1)
    first = (other, left_low, right_low, left_high, right_high)
    first, beside = lax.optimization_barrier((first, beside))
    other, left_low, right_low, left_high, right_high = first
    cross_left, cross_right = across(left_high, 0, 1), across(right_high, 0, 1)
    far_high, far_low = across(right_high, -1), across(left_low, 1)
    next_left, next_right = across(other[:half], 1), across(other[:half], -1)
    whole, far_high = lax.optimization_barrier((whole, far_high))
    lows = [(0, n // 2, 0), (n // 2, m // 2, n)]
    highs = [(0, n // 2, n // 2), (n // 2, m // 2, n + m // 2)]
    both = lows + [(half + source, length, goal) for source, length, goal in highs]
    early = [
        (whole, 0, both), (left_low, 1, lows), (left_high, 1, highs),
        (right_low, 2, lows), (right_high, 2, highs), (other, 4, both),
    ]
    late = [
        (far_low, 3, lows), (far_high, 3, highs),
        (next_left, 5, lows), (cross_left, 5, highs),
        (next_right, 6, lows), (cross_right, 6, highs),
        (across(next_left, 1), 7, lows), (across(far_high, 0, 1), 7, highs),
    ]
    shape = (lax.axis_size("tensor"), n + m, k)
    return put(index, late, shape, put(index, early, shape)), beside


def value_grad_of(total, probs_t_ref, value_ref):
    attn = total.astype(BF16)
    micro_batch, length, depth = probs_t_ref.shape
    head_size = value_ref.shape[1]
    for m in range(micro_batch):
        rows = slice(m * length, (m + 1) * length)
        heads = [
            attn[rows, g * head_size : (g + 1) * head_size] for g in range(depth // length)
        ]
        value_ref[rows, :] = lax.dot_general(
            probs_t_ref[m], jnp.concatenate(heads, 0), NN, preferred_element_type=F32
        ).astype(BF16)


def keep(active, step, steps, first, block, kept, saved_ref, sems):
    def copy(j):
        return pltpu.make_async_copy(kept.at[j], saved_ref.at[first + j], sems.at[j])

    @pl.when(active)
    def _():
        kept[step] = block
        copy(step).start()

    @pl.when(active & (step == steps - 1))
    def _():
        for j in range(steps):
            copy(j).wait()


def plain_kernel(
    steps, section, place_ref, rows_ref, weight_ref, probs_t_ref, kept_ref,
    value_ref, saved_ref, total, kept, sems,
):
    step = pl.program_id(0)

    @pl.when(step == 0)
    def _():
        total[...] = jnp.zeros_like(total)

    total[...] += lax.dot_general(rows_ref[0], weight_ref[...], NN, preferred_element_type=F32)

    @pl.when(step == steps - 1)
    def _():
        value_grad_of(total[...], probs_t_ref, value_ref)

    keep(place_ref[0] == section, step, steps, 0, rows_ref[0], kept, saved_ref, sems)


def turn_kernel(
    first, steps, section, has_total, ends, place_ref, blocks_ref, *refs,
):
    refs = list(refs)
    count = len(steps)
    rows_refs = [refs.pop(0) for _ in range(count)]
    back_ref, weight_ref, probs_t_ref, kept_ref = (refs.pop(0) for _ in range(4))
    total_ref = refs.pop(0) if has_total else None
    new_refs = [refs.pop(0) for _ in range(count)]
    result_ref, saved_ref, heads, total, kept, sems = refs
    step = pl.program_id(0)
    head_size = blocks_ref.shape[2]

    @pl.when(step == 0)
    def _():
        for c in range(blocks_ref.shape[0]):
            heads[:, c * head_size : (c + 1) * head_size] = blocks_ref[c]
        total[...] = total_ref[...] if has_total else jnp.zeros_like(total)

    branch = lax.dot_general(heads[...], back_ref[0], NN, preferred_element_type=F32)

    def finish(rows_ref, new_ref):
        new_rows = (rows_ref[0].astype(F32) + branch).astype(BF16)
        new_ref[0] = new_rows
        total[...] += lax.dot_general(
            new_rows, weight_ref[...], NN, preferred_element_type=F32
        )
        active = place_ref[0] == section
        keep(active, step, sum(steps), first, new_rows, kept, saved_ref, sems)

    if count == 1:
        finish(rows_refs[0], new_refs[0])
    else:
        pl.when(step < steps[0])(lambda: finish(rows_refs[0], new_refs[0]))
        pl.when(step >= steps[0])(lambda: finish(rows_refs[1], new_refs[1]))

    @pl.when(step == sum(steps) - 1)
    def _():
        if ends:
            value_grad_of(total[...], probs_t_ref, result_ref)
        else:
            result_ref[...] = total[...]


def params():
    return pltpu.CompilerParams(vmem_limit_bytes=16 << 20)


def plain_turn(section, place, both, count, weight_t, probs_t, saved):
    steps, length, tile = both.shape
    own = weight_t.shape[1]
    head_size = 128
    return pl.pallas_call(
        functools.partial(plain_kernel, steps, section),
        grid=(steps,),
        in_specs=[
            pl.BlockSpec(memory_space=pltpu.SMEM),
            pl.BlockSpec((1, count, tile), lambda i: (i, length // count - 1, 0)),
            pl.BlockSpec((tile, own), lambda i: (i, 0)),
            pl.BlockSpec(probs_t.shape, lambda i: (0, 0, 0)),
            pl.BlockSpec(memory_space=pl.ANY),
        ],
        out_specs=[
            pl.BlockSpec((count, head_size), lambda i: (0, 0)),
            pl.BlockSpec(memory_space=pl.ANY),
        ],
        out_shape=[
            jax.ShapeDtypeStruct((count, head_size), BF16),
            jax.ShapeDtypeStruct(saved.shape, BF16),
        ],
        scratch_shapes=[
            pltpu.VMEM((count, own), F32),
            pltpu.VMEM((steps, count, tile), BF16),
            pltpu.SemaphoreType.DMA((steps,)),
        ],
        input_output_aliases={4: 1},
        compiler_params=params(),
        cost_estimate=pl.CostEstimate(
            flops=2 * steps * count * tile * own,
            bytes_accessed=2 * steps * tile * own,
            transcendentals=0,
        ),
        name="plain_turn",
    )(place, both, weight_t, probs_t, saved)


def turn(section, place, blocks, rows, back, weight_t, probs_t, saved, first=0, total=None, ends=True):
    count, tile = rows[0].shape[1:]
    own = weight_t.shape[1]
    head_size = blocks.shape[2]
    depth = blocks.shape[0] * head_size
    steps = [part.shape[0] for part in rows]
    parts = [pl.BlockSpec((1, count, tile), lambda i: (jnp.minimum(i, steps[0] - 1), 0, 0))]
    if len(rows) == 2:
        parts.append(
            pl.BlockSpec((1, count, tile), lambda i: (jnp.maximum(i - steps[0], 0), 0, 0))
        )
    whole = pl.BlockSpec((count, own), lambda i: (0, 0))
    extra = [] if total is None else [total]
    if ends:
        result = jax.ShapeDtypeStruct((count, head_size), BF16)
    else:
        result = jax.ShapeDtypeStruct((count, own), F32)
    alias = 5 + len(rows)
    outs = pl.pallas_call(
        functools.partial(turn_kernel, first, steps, section, total is not None, ends),
        grid=(sum(steps),),
        in_specs=[
            pl.BlockSpec(memory_space=pltpu.SMEM),
            pl.BlockSpec(blocks.shape, lambda i: (0, 0, 0)),
            *parts,
            pl.BlockSpec((1, depth, tile), lambda i: (i + first, 0, 0)),
            pl.BlockSpec((tile, own), lambda i: (i + first, 0)),
            pl.BlockSpec(probs_t.shape, lambda i: (0, 0, 0)),
            pl.BlockSpec(memory_space=pl.ANY),
            *[whole for _ in extra],
        ],
        out_specs=[
            *parts,
            pl.BlockSpec(result.shape, lambda i: (0, 0)),
            pl.BlockSpec(memory_space=pl.ANY),
        ],
        out_shape=[
            *[jax.ShapeDtypeStruct(part.shape, BF16) for part in rows],
            result,
            jax.ShapeDtypeStruct(saved.shape, BF16),
        ],
        scratch_shapes=[
            pltpu.VMEM((count, depth), BF16),
            pltpu.VMEM((count, own), F32),
            pltpu.VMEM((sum(steps), count, tile), BF16),
            pltpu.SemaphoreType.DMA((sum(steps),)),
        ],
        input_output_aliases={alias: len(rows) + 1},
        compiler_params=params(),
        cost_estimate=pl.CostEstimate(
            flops=2 * sum(steps) * count * tile * (own + depth),
            bytes_accessed=2 * sum(steps) * tile * (own + depth),
            transcendentals=0,
        ),
        name="turn",
    )(place, blocks, *rows, back, weight_t, probs_t, saved, *extra)
    return outs[:-2], outs[-2], outs[-1]


def pick_kernel(me_ref, rows_ref, out_ref):
    out_ref[...] = rows_ref[0]


def pick(me, rows):
    _, count, tile = rows.shape
    return pl.pallas_call(
        pick_kernel,
        grid_spec=pltpu.PrefetchScalarGridSpec(
            num_scalar_prefetch=1,
            grid=(1,),
            in_specs=[pl.BlockSpec((1, count, tile), lambda i, me: (me[0], 0, 0))],
            out_specs=pl.BlockSpec((count, tile), lambda i, me: (0, 0)),
        ),
        out_shape=jax.ShapeDtypeStruct((count, tile), rows.dtype),
        compiler_params=pltpu.CompilerParams(vmem_limit_bytes=4 << 20),
        name="pick",
    )(me, rows)


def last_kernel(place_ref, me_ref, blocks_ref, rows_ref, value_t_ref, above_ref, out_ref, heads):
    head_size = blocks_ref.shape[2]

    @pl.when(place_ref[0] == 0)
    def _():
        for c in range(blocks_ref.shape[0]):
            heads[:, c * head_size : (c + 1) * head_size] = blocks_ref[c]
        branch = lax.dot_general(heads[...], value_t_ref[...], NN, preferred_element_type=F32)
        out_ref[...] = (rows_ref[0].astype(F32) + branch).astype(BF16)

    @pl.when(place_ref[0] != 0)
    def _():
        out_ref[...] = above_ref[...]


def last_features(place, me, blocks, rows, value_t, above):
    _, count, tile = rows.shape
    depth = value_t.shape[0]
    return pl.pallas_call(
        last_kernel,
        grid_spec=pltpu.PrefetchScalarGridSpec(
            num_scalar_prefetch=2,
            grid=(1,),
            in_specs=[
                pl.BlockSpec(blocks.shape, lambda i, place, me: (0, 0, 0)),
                pl.BlockSpec((1, count, tile), lambda i, place, me: (me[0], 0, 0)),
                pl.BlockSpec(value_t.shape, lambda i, place, me: (0, 0)),
                pl.BlockSpec((count, tile), lambda i, place, me: (0, 0)),
            ],
            out_specs=pl.BlockSpec((count, tile), lambda i, place, me: (0, 0)),
            scratch_shapes=[pltpu.VMEM((count, depth), BF16)],
        ),
        out_shape=jax.ShapeDtypeStruct((count, tile), BF16),
        compiler_params=params(),
        cost_estimate=pl.CostEstimate(
            flops=2 * count * tile * depth, bytes_accessed=2 * tile * depth, transcendentals=0
        ),
        name="last_features",
    )(place, me, blocks, rows, value_t, above)


def weight_kernel(mixed_t_ref, rows_ref, out_ref):
    out_ref[...] = lax.dot_general(
        mixed_t_ref[...], rows_ref[0], NN, preferred_element_type=F32
    ).astype(BF16)


def weight_grads(mixed_t, rows):
    steps, count, tile = rows.shape
    own = mixed_t.shape[0]
    return pl.pallas_call(
        weight_kernel,
        grid=(steps,),
        in_specs=[
            pl.BlockSpec((own, count), lambda i: (0, 0)),
            pl.BlockSpec((1, count, tile), lambda i: (i, 0, 0)),
        ],
        out_specs=pl.BlockSpec((own, tile), lambda i: (0, i)),
        out_shape=jax.ShapeDtypeStruct((own, steps * tile), BF16),
        compiler_params=params(),
        cost_estimate=pl.CostEstimate(
            flops=2 * steps * count * tile * own,
            bytes_accessed=2 * steps * tile * own,
            transcendentals=0,
        ),
        name="weight_grads",
    )(mixed_t, rows)


def on_device(grad_top, query, keys, values, out_weight, value_weight):
    sections = lax.axis_size("section")
    place = lax.axis_index("section")
    me = lax.axis_index("tensor")
    micro_batch, length = query.shape[1], query.shape[2]
    rows = micro_batch * length
    head_size = keys.shape[3]
    group = query.shape[3] // head_size
    feat_local = grad_top.shape[2]
    spot = place.astype(jnp.int32).reshape(1)
    mine = me.astype(jnp.int32).reshape(1)
    xs = lax.axis_size("tensor") // 2
    z, x = me // xs, me % xs
    index = jnp.stack(
        [
            (z + dz) % 2 * xs + (x + dx) % xs
            for dz in (0, 1)
            for dx in (0, -1, 1, 2)
        ]
    ).astype(jnp.int32)
    value_t = transposed(value_weight[0])
    back = lax.ppermute(value_t, "section", [(i, i - 1) for i in range(1, sections)])
    back, index, spot, mine = lax.optimization_barrier((back, index, spot, mine))
    query_heads = query[0].reshape(micro_batch, length, group, head_size)
    probs = jax.vmap(causal_probs)(query_heads, keys[0])
    mixed = jnp.einsum("mgqp,mpd->mqgd", probs, values[0], preferred_element_type=F32)
    mixed_t = transposed(mixed.astype(BF16).reshape(rows, group * head_size), group * head_size)
    probs_t = probs.transpose(0, 3, 1, 2).reshape(micro_batch, length, group * length)
    weight_t = transposed(out_weight[0])
    empty = jnp.zeros((lax.axis_size("tensor"), rows, feat_local), BF16)
    beside = (mixed_t, probs_t, weight_t, value_t, empty)
    both, beside = gather_both(index, back, grad_top.reshape(rows, feat_local), beside)
    mixed_t, probs_t, weight_t, value_t, empty = beside
    value_grad, saved = plain_turn(sections - 1, spot, both, rows, weight_t, probs_t, empty)
    parts = (both[:AHEAD, -rows:], both[AHEAD:, -rows:])
    for section in range(sections - 1, 0, -1):
        moved = hand_down(value_grad, section)
        parts, moved = lax.optimization_barrier((parts, moved))
        parts = [hand_down(part, section) for part in parts]
        blocks = blocks_of_all(moved)
        below = section - 1
        if section % 2:
            parts, value_grad, saved = turn(
                below, spot, blocks, parts, both, weight_t, probs_t, saved
            )
        else:
            (ahead,), total, saved = turn(
                below, spot, blocks, parts[:1], both, weight_t, probs_t, saved, ends=False
            )
            (rest,), value_grad, saved = turn(
                below, spot, blocks, parts[1:], both, weight_t, probs_t, saved, AHEAD, total
            )
            parts = (ahead, rest)
    above = shift(pick(mine, saved), "section", 1)
    grads = last_features(spot, mine, blocks_of_all(value_grad), saved, value_t, above)
    return (
        grads.reshape(1, micro_batch, length, feat_local),
        weight_grads(mixed_t, saved)[None],
    )


def solution(mesh):
    placed = (
        P(None, None, "tensor"),
        P("section", None, None, "tensor"),
        P("section", None, None, "tensor"),
        P("section", None, None, "tensor"),
        P("section", "tensor", None),
        P("section", "tensor", None),
    )
    return jax.shard_map(
        on_device,
        mesh=mesh,
        in_specs=placed,
        out_specs=(P("section", None, None, "tensor"), P("section", "tensor", None)),
        check_vma=False,
    )
```

```python
import functools
import math

import jax
import jax.numpy as jnp
from jax import lax
from jax.experimental import pallas as pl
from jax.experimental.pallas import tpu as pltpu
from jax.sharding import PartitionSpec as P

F32 = jnp.float32
BF16 = jnp.bfloat16
NN = (((1,), (0,)), ((), ()))


AHEAD = 6


def causal_probs(query_heads, key_rows):
    head_size = key_rows.shape[-1]
    length = key_rows.shape[0]
    logits = jnp.einsum("qgd,pd->gqp", query_heads, key_rows, preferred_element_type=F32)
    logits = logits * (1.0 / math.sqrt(head_size))
    row_pos = lax.broadcasted_iota(jnp.int32, (length, length), 0)
    col_pos = lax.broadcasted_iota(jnp.int32, (length, length), 1)
    logits = jnp.where(col_pos <= row_pos, logits, -jnp.inf)
    return jax.nn.softmax(logits, axis=-1).astype(BF16)


def shift(value, axis, by):
    length = lax.axis_size(axis)
    return lax.ppermute(value, axis, [(i, (i + by) % length) for i in range(length)])


def hand_down(value, section):
    length = lax.axis_size("section")
    half = length // 2
    if section % 2:
        pairs = [(i, i ^ 1) for i in range(length)]
    else:
        lows = [section - 1] if section == half else [
            i for i in range(1, length - 1, 2) if i != half - 1
        ]
        other = {i: i for i in range(length)}
        for low in lows:
            other[low], other[low + 1] = low + 1, low
        pairs = sorted(other.items())
    return lax.ppermute(value, "section", pairs)


def copies_kernel(value_ref, out_ref):
    for c in range(out_ref.shape[0]):
        out_ref[c] = value_ref[...]


def blocks_of_all(value):
    shape = (lax.axis_size("tensor"),) + value.shape
    copies = pl.pallas_call(
        copies_kernel,
        in_specs=[pl.BlockSpec(memory_space=pltpu.VMEM)],
        out_specs=pl.BlockSpec(memory_space=pltpu.VMEM),
        out_shape=jax.ShapeDtypeStruct(shape, value.dtype),
        compiler_params=pltpu.CompilerParams(vmem_limit_bytes=6 << 20),
        cost_estimate=pl.CostEstimate(
            flops=0, bytes_accessed=2 * math.prod(shape), transcendentals=0
        ),
        name="copies",
    )(value)
    return lax.all_to_all(copies, "tensor", 0, 0)


def transpose_kernel(value_ref, out_ref):
    out_ref[...] = value_ref[...].T


def transposed(value, tile=512, first=0, count=None):
    rows, columns = value.shape
    count = columns // tile if count is None else count
    return pl.pallas_call(
        transpose_kernel,
        grid=(count,),
        in_specs=[pl.BlockSpec((rows, tile), lambda i: (0, i + first))],
        out_specs=pl.BlockSpec((tile, rows), lambda i: (i, 0)),
        out_shape=jax.ShapeDtypeStruct((count * tile, rows), value.dtype),
        compiler_params=pltpu.CompilerParams(vmem_limit_bytes=12 << 20),
        cost_estimate=pl.CostEstimate(
            flops=0, bytes_accessed=4 * rows * count * tile, transcendentals=0
        ),
        name="transposed",
    )(value)


def place_kernel(spots, given, index_ref, *refs):
    pieces, out_ref, sems = refs[:given], refs[-2], refs[-1]
    copies = []
    for piece, (slot, runs) in zip(pieces, spots):
        for source, length, goal in runs:
            copies.append(
                pltpu.make_async_copy(
                    piece.at[pl.ds(source, length)],
                    out_ref.at[index_ref[slot], pl.ds(goal, length)],
                    sems.at[len(copies)],
                )
            )
    for copy in copies:
        copy.start()
    for copy in copies:
        copy.wait()


def put(index, pieces, shape, whole=None):
    arrays = [piece[0] for piece in pieces]
    spots = [piece[1:] for piece in pieces]
    more = [] if whole is None else [whole]
    return pl.pallas_call(
        functools.partial(place_kernel, spots, len(arrays)),
        in_specs=[pl.BlockSpec(memory_space=pltpu.SMEM)]
        + [pl.BlockSpec(memory_space=pl.ANY)] * (len(arrays) + len(more)),
        out_specs=pl.BlockSpec(memory_space=pl.ANY),
        out_shape=jax.ShapeDtypeStruct(shape, arrays[0].dtype),
        scratch_shapes=[pltpu.SemaphoreType.DMA((sum(len(runs) for _, runs in spots),))],
        input_output_aliases={1 + len(arrays): 0} if more else {},
        compiler_params=pltpu.CompilerParams(vmem_limit_bytes=1 << 20),
        cost_estimate=pl.CostEstimate(
            flops=0,
            bytes_accessed=4 * sum(math.prod(array.shape) for array in arrays),
            transcendentals=0,
        ),
        name="put",
    )(index, *arrays, *more)


def across(value, x_by=0, z_by=0):
    length = lax.axis_size("tensor")
    xs = length // 2
    pairs = []
    for i in range(length):
        z, x = divmod(i, xs)
        pairs.append((i, (z + z_by) % 2 * xs + (x + x_by) % xs))
    return lax.ppermute(value, "tensor", pairs)


def gather_both(index, back, top, beside):
    n, k = back.shape
    m = top.shape[0]
    whole = jnp.concatenate([back[: n // 2], top[: m // 2], back[n // 2 :], top[m // 2 :]])
    whole = lax.optimization_barrier(whole)
    half = (n + m) // 2
    low, high = lax.optimization_barrier((whole[:half], whole[half:]))
    other = across(whole, 0, 1)
    left_low, right_low = across(low, 1), across(low, -1)
    left_high, right_high = across(high, 1), across(high, -1)
    first = (other, left_low, right_low, left_high, right_high)
    first, beside = lax.optimization_barrier((first, beside))
    other, left_low, right_low, left_high, right_high = first
    cross_left, cross_right = across(left_high, 0, 1), across(right_high, 0, 1)
    far_high, far_low = across(right_high, -1), across(left_low, 1)
    next_left, next_right = across(other[:half], 1), across(other[:half], -1)
    whole, far_high = lax.optimization_barrier((whole, far_high))
    lows = [(0, n // 2, 0), (n // 2, m // 2, n)]
    highs = [(0, n // 2, n // 2), (n // 2, m // 2, n + m // 2)]
    both = lows + [(half + source, length, goal) for source, length, goal in highs]
    early = [
        (whole, 0, both), (left_low, 1, lows), (left_high, 1, highs),
        (right_low, 2, lows), (right_high, 2, highs), (other, 4, both),
    ]
    late = [
        (far_low, 3, lows), (far_high, 3, highs),
        (next_left, 5, lows), (cross_left, 5, highs),
        (next_right, 6, lows), (cross_right, 6, highs),
        (across(next_left, 1), 7, lows), (across(far_high, 0, 1), 7, highs),
    ]
    shape = (lax.axis_size("tensor"), n + m, k)
    return put(index, late, shape, put(index, early, shape)), beside


def value_grad_of(total, probs_t_ref, value_ref):
    attn = total.astype(BF16)
    micro_batch, length, depth = probs_t_ref.shape
    head_size = value_ref.shape[1]
    for m in range(micro_batch):
        rows = slice(m * length, (m + 1) * length)
        heads = [
            attn[rows, g * head_size : (g + 1) * head_size] for g in range(depth // length)
        ]
        value_ref[rows, :] = lax.dot_general(
            probs_t_ref[m], jnp.concatenate(heads, 0), NN, preferred_element_type=F32
        ).astype(BF16)


def keep(step, block, saved_ref, sem):
    copy = pltpu.make_async_copy(block, saved_ref.at[step], sem)
    copy.start()
    copy.wait()


def plain_kernel(
    steps, section, place_ref, rows_ref, weight_ref, probs_t_ref, kept_ref,
    value_ref, saved_ref, total, sem,
):
    step = pl.program_id(0)

    @pl.when(step == 0)
    def _():
        total[...] = jnp.zeros_like(total)

    total[...] += lax.dot_general(rows_ref[0], weight_ref[...], NN, preferred_element_type=F32)

    @pl.when(place_ref[0] == section)
    def _():
        keep(step, rows_ref.at[0], saved_ref, sem)

    @pl.when(step == steps - 1)
    def _():
        value_grad_of(total[...], probs_t_ref, value_ref)


def turn_kernel(
    first, steps, section, has_total, ends, place_ref, blocks_ref, *refs,
):
    refs = list(refs)
    count = len(steps)
    rows_refs = [refs.pop(0) for _ in range(count)]
    back_ref, weight_ref, probs_t_ref, kept_ref = (refs.pop(0) for _ in range(4))
    total_ref = refs.pop(0) if has_total else None
    new_refs = [refs.pop(0) for _ in range(count)]
    result_ref, saved_ref, heads, total, sem = refs
    step = pl.program_id(0)
    head_size = blocks_ref.shape[2]

    @pl.when(step == 0)
    def _():
        for c in range(blocks_ref.shape[0]):
            heads[:, c * head_size : (c + 1) * head_size] = blocks_ref[c]
        total[...] = total_ref[...] if has_total else jnp.zeros_like(total)

    branch = lax.dot_general(heads[...], back_ref[0], NN, preferred_element_type=F32)

    def finish(rows_ref, new_ref):
        new_rows = (rows_ref[0].astype(F32) + branch).astype(BF16)
        new_ref[0] = new_rows
        total[...] += lax.dot_general(
            new_rows, weight_ref[...], NN, preferred_element_type=F32
        )

        @pl.when(place_ref[0] == section)
        def _():
            keep(first + step, new_ref.at[0], saved_ref, sem)

    if count == 1:
        finish(rows_refs[0], new_refs[0])
    else:
        pl.when(step < steps[0])(lambda: finish(rows_refs[0], new_refs[0]))
        pl.when(step >= steps[0])(lambda: finish(rows_refs[1], new_refs[1]))

    @pl.when(step == sum(steps) - 1)
    def _():
        if ends:
            value_grad_of(total[...], probs_t_ref, result_ref)
        else:
            result_ref[...] = total[...]


def params():
    return pltpu.CompilerParams(vmem_limit_bytes=16 << 20)


def plain_turn(section, place, both, count, weight_t, probs_t, saved):
    steps, length, tile = both.shape
    own = weight_t.shape[1]
    head_size = 128
    return pl.pallas_call(
        functools.partial(plain_kernel, steps, section),
        grid=(steps,),
        in_specs=[
            pl.BlockSpec(memory_space=pltpu.SMEM),
            pl.BlockSpec((1, count, tile), lambda i: (i, length // count - 1, 0)),
            pl.BlockSpec((tile, own), lambda i: (i, 0)),
            pl.BlockSpec(probs_t.shape, lambda i: (0, 0, 0)),
            pl.BlockSpec(memory_space=pl.ANY),
        ],
        out_specs=[
            pl.BlockSpec((count, head_size), lambda i: (0, 0)),
            pl.BlockSpec(memory_space=pl.ANY),
        ],
        out_shape=[
            jax.ShapeDtypeStruct((count, head_size), BF16),
            jax.ShapeDtypeStruct(saved.shape, BF16),
        ],
        scratch_shapes=[pltpu.VMEM((count, own), F32), pltpu.SemaphoreType.DMA],
        input_output_aliases={4: 1},
        compiler_params=params(),
        cost_estimate=pl.CostEstimate(
            flops=2 * steps * count * tile * own,
            bytes_accessed=2 * steps * tile * own,
            transcendentals=0,
        ),
        name="plain_turn",
    )(place, both, weight_t, probs_t, saved)


def turn(section, place, blocks, rows, back, weight_t, probs_t, saved, first=0, total=None, ends=True):
    count, tile = rows[0].shape[1:]
    own = weight_t.shape[1]
    head_size = blocks.shape[2]
    depth = blocks.shape[0] * head_size
    steps = [part.shape[0] for part in rows]
    parts = [pl.BlockSpec((1, count, tile), lambda i: (jnp.minimum(i, steps[0] - 1), 0, 0))]
    if len(rows) == 2:
        parts.append(
            pl.BlockSpec((1, count, tile), lambda i: (jnp.maximum(i - steps[0], 0), 0, 0))
        )
    whole = pl.BlockSpec((count, own), lambda i: (0, 0))
    extra = [] if total is None else [total]
    if ends:
        result = jax.ShapeDtypeStruct((count, head_size), BF16)
    else:
        result = jax.ShapeDtypeStruct((count, own), F32)
    alias = 5 + len(rows)
    outs = pl.pallas_call(
        functools.partial(turn_kernel, first, steps, section, total is not None, ends),
        grid=(sum(steps),),
        in_specs=[
            pl.BlockSpec(memory_space=pltpu.SMEM),
            pl.BlockSpec(blocks.shape, lambda i: (0, 0, 0)),
            *parts,
            pl.BlockSpec((1, depth, tile), lambda i: (i + first, 0, 0)),
            pl.BlockSpec((tile, own), lambda i: (i + first, 0)),
            pl.BlockSpec(probs_t.shape, lambda i: (0, 0, 0)),
            pl.BlockSpec(memory_space=pl.ANY),
            *[whole for _ in extra],
        ],
        out_specs=[
            *parts,
            pl.BlockSpec(result.shape, lambda i: (0, 0)),
            pl.BlockSpec(memory_space=pl.ANY),
        ],
        out_shape=[
            *[jax.ShapeDtypeStruct(part.shape, BF16) for part in rows],
            result,
            jax.ShapeDtypeStruct(saved.shape, BF16),
        ],
        scratch_shapes=[
            pltpu.VMEM((count, depth), BF16),
            pltpu.VMEM((count, own), F32),
            pltpu.SemaphoreType.DMA,
        ],
        input_output_aliases={alias: len(rows) + 1},
        compiler_params=params(),
        cost_estimate=pl.CostEstimate(
            flops=2 * sum(steps) * count * tile * (own + depth),
            bytes_accessed=2 * sum(steps) * tile * (own + depth),
            transcendentals=0,
        ),
        name="turn",
    )(place, blocks, *rows, back, weight_t, probs_t, saved, *extra)
    return outs[:-2], outs[-2], outs[-1]


def pick_kernel(me_ref, rows_ref, out_ref):
    out_ref[...] = rows_ref[0]


def pick(me, rows):
    _, count, tile = rows.shape
    return pl.pallas_call(
        pick_kernel,
        grid_spec=pltpu.PrefetchScalarGridSpec(
            num_scalar_prefetch=1,
            grid=(1,),
            in_specs=[pl.BlockSpec((1, count, tile), lambda i, me: (me[0], 0, 0))],
            out_specs=pl.BlockSpec((count, tile), lambda i, me: (0, 0)),
        ),
        out_shape=jax.ShapeDtypeStruct((count, tile), rows.dtype),
        compiler_params=pltpu.CompilerParams(vmem_limit_bytes=4 << 20),
        name="pick",
    )(me, rows)


def last_kernel(place_ref, me_ref, blocks_ref, rows_ref, value_t_ref, above_ref, out_ref, heads):
    head_size = blocks_ref.shape[2]

    @pl.when(place_ref[0] == 0)
    def _():
        for c in range(blocks_ref.shape[0]):
            heads[:, c * head_size : (c + 1) * head_size] = blocks_ref[c]
        branch = lax.dot_general(heads[...], value_t_ref[...], NN, preferred_element_type=F32)
        out_ref[...] = (rows_ref[0].astype(F32) + branch).astype(BF16)

    @pl.when(place_ref[0] != 0)
    def _():
        out_ref[...] = above_ref[...]


def last_features(place, me, blocks, rows, value_t, above):
    _, count, tile = rows.shape
    depth = value_t.shape[0]
    return pl.pallas_call(
        last_kernel,
        grid_spec=pltpu.PrefetchScalarGridSpec(
            num_scalar_prefetch=2,
            grid=(1,),
            in_specs=[
                pl.BlockSpec(blocks.shape, lambda i, place, me: (0, 0, 0)),
                pl.BlockSpec((1, count, tile), lambda i, place, me: (me[0], 0, 0)),
                pl.BlockSpec(value_t.shape, lambda i, place, me: (0, 0)),
                pl.BlockSpec((count, tile), lambda i, place, me: (0, 0)),
            ],
            out_specs=pl.BlockSpec((count, tile), lambda i, place, me: (0, 0)),
            scratch_shapes=[pltpu.VMEM((count, depth), BF16)],
        ),
        out_shape=jax.ShapeDtypeStruct((count, tile), BF16),
        compiler_params=params(),
        cost_estimate=pl.CostEstimate(
            flops=2 * count * tile * depth, bytes_accessed=2 * tile * depth, transcendentals=0
        ),
        name="last_features",
    )(place, me, blocks, rows, value_t, above)


def weight_kernel(mixed_t_ref, rows_ref, out_ref):
    out_ref[...] = lax.dot_general(
        mixed_t_ref[...], rows_ref[0], NN, preferred_element_type=F32
    ).astype(BF16)


def weight_grads(mixed_t, rows):
    steps, count, tile = rows.shape
    own = mixed_t.shape[0]
    return pl.pallas_call(
        weight_kernel,
        grid=(steps,),
        in_specs=[
            pl.BlockSpec((own, count), lambda i: (0, 0)),
            pl.BlockSpec((1, count, tile), lambda i: (i, 0, 0)),
        ],
        out_specs=pl.BlockSpec((own, tile), lambda i: (0, i)),
        out_shape=jax.ShapeDtypeStruct((own, steps * tile), BF16),
        compiler_params=params(),
        cost_estimate=pl.CostEstimate(
            flops=2 * steps * count * tile * own,
            bytes_accessed=2 * steps * tile * own,
            transcendentals=0,
        ),
        name="weight_grads",
    )(mixed_t, rows)


def on_device(grad_top, query, keys, values, out_weight, value_weight):
    sections = lax.axis_size("section")
    place = lax.axis_index("section")
    me = lax.axis_index("tensor")
    micro_batch, length = query.shape[1], query.shape[2]
    rows = micro_batch * length
    head_size = keys.shape[3]
    group = query.shape[3] // head_size
    feat_local = grad_top.shape[2]
    spot = place.astype(jnp.int32).reshape(1)
    mine = me.astype(jnp.int32).reshape(1)
    xs = lax.axis_size("tensor") // 2
    z, x = me // xs, me % xs
    index = jnp.stack(
        [
            (z + dz) % 2 * xs + (x + dx) % xs
            for dz in (0, 1)
            for dx in (0, -1, 1, 2)
        ]
    ).astype(jnp.int32)
    value_t = transposed(value_weight[0])
    back = lax.ppermute(value_t, "section", [(i, i - 1) for i in range(1, sections)])
    back, index, spot, mine = lax.optimization_barrier((back, index, spot, mine))
    query_heads = query[0].reshape(micro_batch, length, group, head_size)
    probs = jax.vmap(causal_probs)(query_heads, keys[0])
    mixed = jnp.einsum("mgqp,mpd->mqgd", probs, values[0], preferred_element_type=F32)
    mixed_t = transposed(mixed.astype(BF16).reshape(rows, group * head_size), group * head_size)
    probs_t = probs.transpose(0, 3, 1, 2).reshape(micro_batch, length, group * length)
    weight_t = transposed(out_weight[0])
    empty = jnp.zeros((lax.axis_size("tensor"), rows, feat_local), BF16)
    beside = (mixed_t, probs_t, weight_t, value_t, empty)
    both, beside = gather_both(index, back, grad_top.reshape(rows, feat_local), beside)
    mixed_t, probs_t, weight_t, value_t, empty = beside
    value_grad, saved = plain_turn(sections - 1, spot, both, rows, weight_t, probs_t, empty)
    parts = (both[:AHEAD, -rows:], both[AHEAD:, -rows:])
    for section in range(sections - 1, 0, -1):
        moved = hand_down(value_grad, section)
        parts, moved = lax.optimization_barrier((parts, moved))
        parts = [hand_down(part, section) for part in parts]
        blocks = blocks_of_all(moved)
        below = section - 1
        if section % 2:
            parts, value_grad, saved = turn(
                below, spot, blocks, parts, both, weight_t, probs_t, saved
            )
        else:
            (ahead,), total, saved = turn(
                below, spot, blocks, parts[:1], both, weight_t, probs_t, saved, ends=False
            )
            (rest,), value_grad, saved = turn(
                below, spot, blocks, parts[1:], both, weight_t, probs_t, saved, AHEAD, total
            )
            parts = (ahead, rest)
    above = shift(pick(mine, saved), "section", 1)
    grads = last_features(spot, mine, blocks_of_all(value_grad), saved, value_t, above)
    return (
        grads.reshape(1, micro_batch, length, feat_local),
        weight_grads(mixed_t, saved)[None],
    )


def solution(mesh):
    placed = (
        P(None, None, "tensor"),
        P("section", None, None, "tensor"),
        P("section", None, None, "tensor"),
        P("section", None, None, "tensor"),
        P("section", "tensor", None),
        P("section", "tensor", None),
    )
    return jax.shard_map(
        on_device,
        mesh=mesh,
        in_specs=placed,
        out_specs=(P("section", None, None, "tensor"), P("section", "tensor", None)),
        check_vma=False,
    )
```
